32 devices in a mesh: groups: 2 (over y), bins: 16 (over z, x, core).
Axes of the slice: x: 2, y: 2, z: 4, core: 2. Of those that a mesh axis runs over, the one named last changes fastest.
Arguments:
- snapshots: bfloat16 [256, 32, 2, 256], P(('groups', 'bins')), parts along dimension 0, may hold values from -6 to 6
- directions: float32 [64, 2, 2048], P('groups'), parts along dimension 0, may hold values from -0.7 to 0.7
- positions: float32 [2, 256], replicated, may hold values from -6 to 6
- look_counts: int32 [64], P('groups'), parts along dimension 0, may hold values from 1 to 2048, as said below
- bin_order: int32 [64], P('groups'), parts along dimension 0, may hold values from 0 to 31, as said below
Outputs:
- power_map: float32 [64, 2048], P(('groups', 'bins')), parts along dimension 0
The draws below stay inside these ranges and needn't reach their ends.
There are 2 independent parts, one for each index of `groups`. The reference program is written for one: setup_inputs(seed, part) draws one part's arguments, and reference() takes and returns one part's arrays. A program takes and returns all parts, laid end to end along the dimension named above; an argument that names none is the same for every part. Nothing has to cross between parts.
Inputs may be any that keep to these rules, and one draw needn't show every extreme that they name: `look_counts`: the number of looks imaged in each bin; some bin images all 2048. `bin_order`: a permutation of the 32 bins.
All inputs are finite; a program needn't handle non-finite values.
Results may differ from the reference program's by a relative error of at most 0.0003.
Values may be sent and summed in bfloat16 or wider, within the bound.
A program may use at most 64 MiB of HBM per device.

```python
import math
import jax
import jax.numpy as jnp
from jax import lax

SENSORS = 256
LOOKS = 2048
BIN_DEV = 2
BINS = 32
SNAP = 128


def plan(key):
    devices = BINS // BIN_DEV
    key_level, key_count, key_full = jax.random.split(key, 3)
    levels = jax.random.randint(key_level, (devices,), 1, 5)
    ceiling = jnp.maximum(LOOKS * jnp.repeat(levels * levels, BIN_DEV) // 16, 1)
    draws_raw = jax.random.randint(key_count, (BINS,), 0, LOOKS)
    counts = 1 + draws_raw % ceiling
    chosen = jax.random.randint(key_full, (), 0, BINS)
    indices = jnp.arange(BINS, dtype=jnp.int32)
    counts = jnp.where(indices == chosen, LOOKS, counts).astype(jnp.int32)
    scores = counts * BINS + indices
    ranked = jnp.argsort(-scores).astype(jnp.int32)
    rounds = indices // devices
    within = indices % devices
    target = jnp.where(rounds % 2 == 0, within, devices - 1 - within)
    slot_row = target * BIN_DEV + rounds
    order = jnp.zeros((BINS,), jnp.int32).at[slot_row].set(ranked)
    return (counts, order)


def draw_look_counts(key, part):
    counts, order = plan(key)
    return counts


def draw_bin_order(key, part):
    counts, order = plan(key)
    return order


def block_levels(rng, dims, shards, low, largest):
    level = 1.0
    for position, shards_of in shards:
        draws = jax.random.uniform(jax.random.fold_in(jax.random.fold_in(rng, 6), position), (shards_of,), jnp.float32, low / len(shards), largest / len(shards))
        level = level * jnp.repeat(jnp.exp(draws), dims[position] // shards_of).reshape((-1,) + (1,) * (len(dims) - 1 - position))
    return level


def centred(own_key, extent, spread, limit, pieces=(), kind=jnp.bfloat16):
    entries = spread * jax.random.normal(own_key, extent, jnp.float32)
    if pieces:
        entries = entries * block_levels(own_key, extent, pieces, -0.22, 0.18)
    return jnp.clip(entries, -limit, limit).astype(kind)


def setup_inputs(seed: int = 0, part: int = 0) -> dict:
    key_list = jax.random.split(jax.random.key(seed), 6)
    own_keys = jax.random.split(jax.random.fold_in(key_list[5], part), 6)
    snapshots = centred(own_keys[0], (SNAP, BINS, 2, SENSORS), 0.7, 6.0, ((0, 16),))
    directions = jnp.clip(jax.random.uniform(own_keys[1], (BINS, 2, LOOKS), jnp.float32, -0.7, 0.7), -0.7, 0.7)
    positions = jnp.clip(jax.random.uniform(key_list[2], (2, SENSORS), jnp.float32, -6.0, 6.0), -6.0, 6.0)
    look_counts = draw_look_counts(jax.random.fold_in(jax.random.fold_in(key_list[5], part), 71), part)
    bin_order = draw_bin_order(jax.random.fold_in(jax.random.fold_in(key_list[5], part), 71), part)
    return {"snapshots": snapshots, "directions": directions, "positions": positions, "look_counts": look_counts, "bin_order": bin_order}


def bin_power(snapshots, directions, positions, look_counts, bin_id):
    stacked = lax.dynamic_index_in_dim(snapshots, bin_id, 1, keepdims=False).reshape(SNAP, 2 * SENSORS)
    products = jnp.dot(stacked.T.astype(jnp.float32), stacked.astype(jnp.float32), preferred_element_type=jnp.float32)
    real_cov = (products[:SENSORS, :SENSORS] + products[SENSORS:, SENSORS:]) / SNAP
    imag_cov = (products[SENSORS:, :SENSORS] - products[:SENSORS, SENSORS:]) / SNAP
    embedded = jnp.concatenate([jnp.concatenate([real_cov, -imag_cov], 1), jnp.concatenate([imag_cov, real_cov], 1)], 0)
    embedded = embedded + 0.1 * jnp.eye(2 * SENSORS, dtype=jnp.float32)
    factor = jnp.linalg.cholesky(embedded)
    angles = lax.dynamic_index_in_dim(directions, bin_id, 0, keepdims=False)
    freq_ratio = 0.5 + (bin_id.astype(jnp.float32) + 0.5) / BINS
    phases = 2.0 * math.pi * freq_ratio * (positions[0][:, None] * angles[0][None, :] + positions[1][:, None] * angles[1][None, :])
    steering = jnp.concatenate([jnp.cos(phases), -jnp.sin(phases)], 0)
    whitened = lax.linalg.triangular_solve(factor, steering, left_side=True, lower=True)
    quadratic = jnp.sum(whitened * whitened, 0)
    look_count = lax.dynamic_index_in_dim(look_counts, bin_id, 0, keepdims=False)
    return jnp.where(jnp.arange(LOOKS, dtype=jnp.int32) < look_count, SENSORS / quadratic, jnp.zeros_like(quadratic))

def reference(snapshots, directions, positions, look_counts, bin_order):
    return lax.map(lambda bin_id: bin_power(snapshots, directions, positions, look_counts, bin_id), bin_order)
```

```python
import functools
import math

import jax
import jax.numpy as jnp
from jax import lax
from jax.experimental import pallas as pl
from jax.experimental.pallas import tpu as pltpu
from jax.sharding import PartitionSpec as P

LOOK_BLK = 128
LOADING = 0.1
PIVOT = 32
WIDE = 256
COS_TERMS = (6.528658390045166, -25.967599868774414, 60.16762924194336, -85.45014190673828,
             64.93911743164062, -19.73920440673828, 1.0)
SIN_TERMS = (3.2381374835968018, -14.899847030639648, 42.02592849731445, -76.70301818847656,
             81.60513305664062, -41.34170150756836, 6.2831854820251465)
F32 = jnp.float32
BF16 = jnp.bfloat16


def mm(a, b, dims=((1,), (0,)), exact=False):
    precision = lax.Precision.HIGHEST if exact else None
    return lax.dot_general(a, b, (dims, ((), ())), precision=precision, preferred_element_type=F32)


def halves(x):
    high = x.astype(BF16)
    return high, (x - high.astype(F32)).astype(BF16)


def polynomial(z, terms):
    value = z * terms[0] + terms[1]
    for term in terms[2:]:
        value = value * z + term
    return value


def invert_small(blocks):
    n = blocks[0][0].shape[0]
    rows = lax.broadcasted_iota(jnp.int32, (n, n), 0)
    cols = lax.broadcasted_iota(jnp.int32, (n, n), 1)
    one_row = lax.broadcasted_iota(jnp.int32, (1, n), 1)
    blocks = list(blocks)
    for k in range(n):
        for i, (re, im) in enumerate(blocks):
            scale = 1.0 / re[k : k + 1, k : k + 1]
            row_re = jnp.where(one_row == k, 1.0, re[k : k + 1, :]) * scale
            row_im = jnp.where(one_row == k, 0.0, im[k : k + 1, :]) * scale
            col_re = re[:, k : k + 1]
            col_im = im[:, k : k + 1]
            rest_re = jnp.where(cols == k, 0.0, re)
            rest_im = jnp.where(cols == k, 0.0, im)
            next_re = rest_re - col_re * row_re + col_im * row_im
            next_im = rest_im - col_re * row_im - col_im * row_re
            blocks[i] = (
                jnp.where(rows == k, row_re, next_re),
                jnp.where(rows == k, row_im, next_im),
            )
    return blocks


def put_rows(whole, rows, start):
    stop = start + rows.shape[0]
    pieces = [rows]
    if start:
        pieces.insert(0, whole[:start])
    if stop < whole.shape[0]:
        pieces.append(whole[stop:])
    return jnp.concatenate(pieces, 0)


def invert(mats):
    n = mats[0][0].shape[0]
    mats = list(mats)
    for start in range(0, n, PIVOT):
        stop = start + PIVOT
        small = invert_small([(re[start:stop, start:stop], im[start:stop, start:stop]) for re, im in mats])
        cols = lax.broadcasted_iota(jnp.int32, (n, n), 1)
        inside = (cols >= start) & (cols < stop)
        unit = lax.broadcasted_iota(jnp.int32, (PIVOT, n), 0) + start == lax.broadcasted_iota(
            jnp.int32, (PIVOT, n), 1
        )
        band = inside[:PIVOT]
        for i, (re, im) in enumerate(mats):
            row_re = jnp.where(band, unit.astype(F32), re[start:stop])
            row_im = jnp.where(band, 0.0, im[start:stop])
            d_re, d_im = small[i]
            both = jnp.concatenate([row_re, row_im], 1)
            p = mm(d_re, both, exact=True)
            q = mm(d_im, both, exact=True)
            t_re = p[:, :n] - q[:, n:]
            t_im = p[:, n:] + q[:, :n]
            both = jnp.concatenate([t_re, t_im], 1)
            p = mm(re[:, start:stop], both, exact=True)
            q = mm(im[:, start:stop], both, exact=True)
            next_re = jnp.where(inside, 0.0, re) - p[:, :n] + q[:, n:]
            next_im = jnp.where(inside, 0.0, im) - p[:, n:] - q[:, :n]
            mats[i] = (put_rows(next_re, t_re, start), put_rows(next_im, t_im, start))
    return mats


def image_kernel(per_device, total_bins, order_ref, counts_ref, snaps_ref, directions_ref, spots_ref, out_ref,
                 solver_ref, turned_ref, spot_ref):
    first = lax.axis_index("bins") * per_device
    snap = snaps_ref.shape[0] // per_device
    sensors = spots_ref.shape[0]
    looks = out_ref.shape[1]
    ridge = LOADING * snap
    both = snaps_ref[...].astype(F32).reshape(snap // 8, per_device, 8, 2 * sensors)
    diag = lax.broadcasted_iota(jnp.int32, (snap, snap), 0) == lax.broadcasted_iota(jnp.int32, (snap, snap), 1)
    mats, fields = [], []
    for local in range(per_device):
        data = both[:, local].reshape(snap, 2 * sensors)
        turned = jnp.concatenate([-data[:, sensors:], data[:, :sensors]], 1)
        top, low = data.astype(BF16), turned.astype(BF16)
        gram_re = mm(top, top, ((1,), (1,)))
        gram_im = mm(low, top, ((1,), (1,)))
        mats.append((gram_re + jnp.where(diag, ridge, 0.0), gram_im))
        fields.append((top, low))
        turned_ref[local] = jnp.concatenate([data, turned], 0).T.astype(BF16)
    mats = invert(mats)
    for local in range(per_device):
        re, im = mats[local]
        stacked = jnp.concatenate(fields[local], 0)
        high, low = halves(jnp.concatenate([re, -im], 1))
        upper = mm(high, stacked) + mm(low, stacked)
        lower = jnp.concatenate([-upper[:, sensors:], upper[:, :sensors]], 1)
        high, low = halves(jnp.concatenate([upper, lower], 0))
        solver_ref[local, 0] = high
        solver_ref[local, 1] = low
    out_ref[...] = jnp.zeros_like(out_ref)
    for local in range(per_device):
        bin_id = order_ref[first + local]
        count = counts_ref[bin_id]
        ratio = 0.5 + (bin_id.astype(F32) + 0.5) / total_bins
        spot_ref[0] = jnp.broadcast_to(spots_ref[:, 0:1] * ratio, (sensors, 128))
        spot_ref[1] = jnp.broadcast_to(spots_ref[:, 1:2] * ratio, (sensors, 128))

        def one_block(block, carry):
            offset = pl.multiple_of(block * WIDE, WIDE)
            piece = directions_ref[bin_id, :, pl.ds(offset, WIDE)]
            x = jnp.concatenate([spot_ref[0]] * (WIDE // 128), 1)
            y = jnp.concatenate([spot_ref[1]] * (WIDE // 128), 1)
            turns = x * piece[0:1] + y * piece[1:2]
            turns = turns - jnp.round(turns)
            z = turns * turns
            cosine = polynomial(z, COS_TERMS)
            sine = polynomial(z, SIN_TERMS) * turns
            steering = jnp.concatenate([cosine, -sine], 0)
            s_high, s_low = halves(steering)
            weights = mm(solver_ref[local, 0], s_high) + mm(solver_ref[local, 1], s_high) + mm(solver_ref[local, 0], s_low)
            w_high, w_low = halves(weights)
            fitted = mm(turned_ref[local], w_high) + mm(turned_ref[local], w_low)
            left = steering - fitted
            power = jnp.sum(left * left, 0, keepdims=True) + ridge * jnp.sum(weights * weights, 0, keepdims=True)
            index = offset + lax.broadcasted_iota(jnp.int32, (1, WIDE), 1)
            out_ref[local : local + 1, pl.ds(offset, WIDE)] = jnp.where(index < count, LOADING * sensors / power, 0.0)
            return carry

        lax.fori_loop(0, (count + WIDE - 1) // WIDE, one_block, 0)


def few_snapshots(snapshots, directions, positions, look_counts, bin_order):
    devices = lax.axis_size("bins")
    block, total_bins, _, sensors = snapshots.shape
    per_device = total_bins // devices
    looks = directions.shape[2]
    ordered = jnp.take(snapshots.reshape(block, total_bins, 2 * sensors), bin_order, axis=1)
    ordered = ordered.transpose(1, 0, 2).reshape(devices, per_device * block, 2 * sensors)
    arrived = lax.all_to_all(ordered, "bins", split_axis=0, concat_axis=0, tiled=True)
    arrived = arrived.reshape(devices * per_device * block, 2 * sensors)
    snap = devices * block
    smem = pl.BlockSpec(memory_space=pltpu.SMEM)
    vmem = pl.BlockSpec(memory_space=pltpu.VMEM)
    return pl.pallas_call(
        functools.partial(image_kernel, per_device, total_bins),
        out_shape=jax.ShapeDtypeStruct((per_device, looks), F32),
        in_specs=[smem, smem, vmem, vmem, vmem],
        out_specs=vmem,
        scratch_shapes=[
            pltpu.VMEM((per_device, 2, 2 * snap, 2 * sensors), BF16),
            pltpu.VMEM((per_device, 2 * sensors, 2 * snap), BF16),
            pltpu.VMEM((2, sensors, 128), F32),
        ],
        compiler_params=pltpu.CompilerParams(vmem_limit_bytes=40 * 1024 * 1024),
    )(bin_order, look_counts, arrived, directions, positions.T)


def image_bin(stacked, angles, positions, look_count, bin_id, total_bins):
    sensors = positions.shape[1]
    snap_total = stacked.shape[0]
    looks = angles.shape[1]
    products = lax.dot_general(
        stacked, stacked, (((0,), (0,)), ((), ())), preferred_element_type=jnp.float32
    )
    real_cov = (products[:sensors, :sensors] + products[sensors:, sensors:]) / snap_total
    imag_cov = (products[sensors:, :sensors] - products[:sensors, sensors:]) / snap_total
    embedded = jnp.concatenate(
        [jnp.concatenate([real_cov, -imag_cov], 1), jnp.concatenate([imag_cov, real_cov], 1)], 0
    )
    identity = jnp.eye(2 * sensors, dtype=jnp.float32)
    factor = jnp.linalg.cholesky(embedded + 0.1 * identity)
    inverse = lax.linalg.triangular_solve(factor, identity, left_side=True, lower=True)
    freq_ratio = 0.5 + (bin_id.astype(jnp.float32) + 0.5) / total_bins
    active = (look_count + LOOK_BLK - 1) // LOOK_BLK

    def one_block(block, powers):
        offset = block * LOOK_BLK
        piece = lax.dynamic_slice_in_dim(angles, offset, LOOK_BLK, 1)
        phases = (
            2.0
            * math.pi
            * freq_ratio
            * (
                positions[0][:, None] * piece[0][None, :]
                + positions[1][:, None] * piece[1][None, :]
            )
        )
        steering = jnp.concatenate([jnp.cos(phases), -jnp.sin(phases)], 0)
        whitened = jnp.dot(
            inverse, steering, precision=lax.Precision.HIGHEST, preferred_element_type=jnp.float32
        )
        quadratic = jnp.sum(whitened * whitened, 0)
        look_index = offset + jnp.arange(LOOK_BLK, dtype=jnp.int32)
        values = jnp.where(look_index < look_count, sensors / quadratic, jnp.zeros_like(quadratic))
        return lax.dynamic_update_slice_in_dim(powers, values, offset, 0)

    return lax.fori_loop(0, active, one_block, jnp.zeros((looks,), jnp.float32))


def many_snapshots(snapshots, directions, positions, look_counts, bin_order):
    devices = lax.axis_size("bins")
    device = lax.axis_index("bins")
    total_bins = snapshots.shape[1]
    per_device = total_bins // devices
    sensors = snapshots.shape[3]
    bin_ids = device * per_device + jnp.arange(per_device, dtype=jnp.int32)
    turned = lax.all_to_all(snapshots, "bins", split_axis=1, concat_axis=0, tiled=True)
    snap_total = turned.shape[0]
    rows = []
    for local in range(per_device):
        bin_id = bin_ids[local]
        stacked = turned[:, local].reshape(snap_total, 2 * sensors)
        angles = lax.dynamic_index_in_dim(directions, bin_id, 0, keepdims=False)
        look_count = lax.dynamic_index_in_dim(look_counts, bin_id, 0, keepdims=False)
        rows.append(image_bin(stacked, angles, positions, look_count, bin_id, total_bins))
    powers = jnp.stack(rows, 0)
    whole = lax.all_gather(powers, "bins", axis=0, tiled=True)
    my_rows = lax.dynamic_slice_in_dim(bin_order, device * per_device, per_device)
    powers = jnp.take(whole, my_rows, axis=0)
    return powers


def body(snapshots, directions, positions, look_counts, bin_order):
    snap_total = snapshots.shape[0] * lax.axis_size("bins")
    form = few_snapshots if snap_total < snapshots.shape[3] else many_snapshots
    return form(snapshots, directions, positions, look_counts, bin_order)


def solution(mesh):
    placed = (
        P(("groups", "bins"), None, None, None),
        P("groups", None, None),
        P(),
        P("groups"),
        P("groups"),
    )
    return jax.shard_map(
        body, mesh=mesh, in_specs=placed, out_specs=P(("groups", "bins"), None), check_vma=False
    )
```

```python
import functools
import math

import jax
import jax.numpy as jnp
from jax import lax
from jax.experimental import pallas as pl
from jax.experimental.pallas import tpu as pltpu
from jax.sharding import PartitionSpec as P

LOOK_BLK = 128
LOADING = 0.1
PIVOT = 32
WIDE = 512
COS_TERMS = (6.528658390045166, -25.967599868774414, 60.16762924194336, -85.45014190673828,
             64.93911743164062, -19.73920440673828, 1.0)
SIN_TERMS = (3.2381374835968018, -14.899847030639648, 42.02592849731445, -76.70301818847656,
             81.60513305664062, -41.34170150756836, 6.2831854820251465)
F32 = jnp.float32
BF16 = jnp.bfloat16


def mm(a, b, dims=((1,), (0,)), exact=False):
    precision = lax.Precision.HIGHEST if exact else None
    return lax.dot_general(a, b, (dims, ((), ())), precision=precision, preferred_element_type=F32)


def halves(x):
    high = x.astype(BF16)
    return high, (x - high.astype(F32)).astype(BF16)


def polynomial(z, terms):
    value = z * terms[0] + terms[1]
    for term in terms[2:]:
        value = value * z + term
    return value


def invert_small(blocks):
    n = blocks[0][0].shape[0]
    rows = lax.broadcasted_iota(jnp.int32, (n, n), 0)
    cols = lax.broadcasted_iota(jnp.int32, (n, n), 1)
    one_row = lax.broadcasted_iota(jnp.int32, (1, n), 1)
    blocks = list(blocks)
    for k in range(n):
        for i, (re, im) in enumerate(blocks):
            scale = 1.0 / re[k : k + 1, k : k + 1]
            row_re = jnp.where(one_row == k, 1.0, re[k : k + 1, :]) * scale
            row_im = jnp.where(one_row == k, 0.0, im[k : k + 1, :]) * scale
            col_re = re[:, k : k + 1]
            col_im = im[:, k : k + 1]
            rest_re = jnp.where(cols == k, 0.0, re)
            rest_im = jnp.where(cols == k, 0.0, im)
            next_re = rest_re - col_re * row_re + col_im * row_im
            next_im = rest_im - col_re * row_im - col_im * row_re
            blocks[i] = (
                jnp.where(rows == k, row_re, next_re),
                jnp.where(rows == k, row_im, next_im),
            )
    return blocks


def put_rows(whole, rows, start):
    stop = start + rows.shape[0]
    pieces = [rows]
    if start:
        pieces.insert(0, whole[:start])
    if stop < whole.shape[0]:
        pieces.append(whole[stop:])
    return jnp.concatenate(pieces, 0)


def invert(mats):
    n = mats[0][0].shape[0]
    mats = list(mats)
    for start in range(0, n, PIVOT):
        stop = start + PIVOT
        small = invert_small([(re[start:stop, start:stop], im[start:stop, start:stop]) for re, im in mats])
        cols = lax.broadcasted_iota(jnp.int32, (n, n), 1)
        inside = (cols >= start) & (cols < stop)
        unit = lax.broadcasted_iota(jnp.int32, (PIVOT, n), 0) + start == lax.broadcasted_iota(
            jnp.int32, (PIVOT, n), 1
        )
        band = inside[:PIVOT]
        for i, (re, im) in enumerate(mats):
            row_re = jnp.where(band, unit.astype(F32), re[start:stop])
            row_im = jnp.where(band, 0.0, im[start:stop])
            d_re, d_im = small[i]
            both = jnp.concatenate([row_re, row_im], 1)
            p = mm(d_re, both, exact=True)
            q = mm(d_im, both, exact=True)
            t_re = p[:, :n] - q[:, n:]
            t_im = p[:, n:] + q[:, :n]
            both = jnp.concatenate([t_re, t_im], 1)
            p = mm(re[:, start:stop], both, exact=True)
            q = mm(im[:, start:stop], both, exact=True)
            next_re = jnp.where(inside, 0.0, re) - p[:, :n] + q[:, n:]
            next_im = jnp.where(inside, 0.0, im) - p[:, n:] - q[:, :n]
            mats[i] = (put_rows(next_re, t_re, start), put_rows(next_im, t_im, start))
    return mats


def image_kernel(per_device, total_bins, order_ref, counts_ref, snaps_ref, directions_ref, spots_ref, out_ref,
                 solver_ref, turned_ref, spot_ref):
    first = lax.axis_index("bins") * per_device
    snap = snaps_ref.shape[0] // per_device
    sensors = spots_ref.shape[0]
    looks = out_ref.shape[1]
    ridge = LOADING * snap
    both = snaps_ref[...].astype(F32).reshape(snap // 8, per_device, 8, 2 * sensors)
    diag = lax.broadcasted_iota(jnp.int32, (snap, snap), 0) == lax.broadcasted_iota(jnp.int32, (snap, snap), 1)
    mats, fields = [], []
    for local in range(per_device):
        data = both[:, local].reshape(snap, 2 * sensors)
        turned = jnp.concatenate([-data[:, sensors:], data[:, :sensors]], 1)
        top, low = data.astype(BF16), turned.astype(BF16)
        gram_re = mm(top, top, ((1,), (1,)))
        gram_im = mm(low, top, ((1,), (1,)))
        mats.append((gram_re + jnp.where(diag, ridge, 0.0), gram_im))
        fields.append((top, low))
        turned_ref[local] = jnp.concatenate([data, turned], 0).T.astype(BF16)
    mats = invert(mats)
    for local in range(per_device):
        re, im = mats[local]
        stacked = jnp.concatenate(fields[local], 0)
        high, low = halves(jnp.concatenate([re, -im], 1))
        upper = mm(high, stacked) + mm(low, stacked)
        lower = jnp.concatenate([-upper[:, sensors:], upper[:, :sensors]], 1)
        high, low = halves(jnp.concatenate([upper, lower], 0))
        solver_ref[local, 0] = high
        solver_ref[local, 1] = low
    out_ref[...] = jnp.zeros_like(out_ref)
    for local in range(per_device):
        bin_id = order_ref[first + local]
        count = counts_ref[bin_id]
        ratio = 0.5 + (bin_id.astype(F32) + 0.5) / total_bins
        spot_ref[0] = jnp.broadcast_to(spots_ref[:, 0:1] * ratio, (sensors, 128))
        spot_ref[1] = jnp.broadcast_to(spots_ref[:, 1:2] * ratio, (sensors, 128))

        def one_block(block, carry):
            offset = pl.multiple_of(block * WIDE, WIDE)
            piece = directions_ref[bin_id, :, pl.ds(offset, WIDE)]
            x = jnp.concatenate([spot_ref[0]] * (WIDE // 128), 1)
            y = jnp.concatenate([spot_ref[1]] * (WIDE // 128), 1)
            turns = x * piece[0:1] + y * piece[1:2]
            turns = turns - jnp.round(turns)
            z = turns * turns
            cosine = polynomial(z, COS_TERMS)
            sine = polynomial(z, SIN_TERMS) * turns
            steering = jnp.concatenate([cosine, -sine], 0)
            s_high, s_low = halves(steering)
            weights = mm(solver_ref[local, 0], s_high) + mm(solver_ref[local, 1], s_high) + mm(solver_ref[local, 0], s_low)
            w_high, w_low = halves(weights)
            fitted = mm(turned_ref[local], w_high) + mm(turned_ref[local], w_low)
            left = steering - fitted
            power = jnp.sum(left * left, 0, keepdims=True) + ridge * jnp.sum(weights * weights, 0, keepdims=True)
            index = offset + lax.broadcasted_iota(jnp.int32, (1, WIDE), 1)
            out_ref[local : local + 1, pl.ds(offset, WIDE)] = jnp.where(index < count, LOADING * sensors / power, 0.0)
            return carry

        lax.fori_loop(0, (count + WIDE - 1) // WIDE, one_block, 0)


def exchange_kernel(devices, per_device, order_ref, snaps_ref, out_ref, send_ref, send_sem, recv_sem, own_sem):
    me = lax.axis_index("bins")
    barrier = pltpu.get_barrier_semaphore()

    def greet(step, carry):
        peer = lax.rem(me + step, devices)
        pl.semaphore_signal(barrier, inc=1, device_id={"bins": peer}, device_id_type=pl.DeviceIdType.MESH)
        return carry

    lax.fori_loop(1, devices, greet, 0)
    for owner in range(devices):
        pieces = [snaps_ref[order_ref[owner * per_device + local]].astype(F32) for local in range(per_device)]
        send_ref[owner] = jnp.concatenate(pieces, 0).astype(BF16)
    own = pltpu.make_async_copy(send_ref.at[me], out_ref.at[me], own_sem)
    own.start()
    pl.semaphore_wait(barrier, devices - 1)

    def copy(step):
        peer = lax.rem(me + step, devices)
        return pltpu.make_async_remote_copy(
            src_ref=send_ref.at[peer],
            dst_ref=out_ref.at[me],
            send_sem=send_sem.at[step],
            recv_sem=recv_sem.at[step],
            device_id={"bins": peer},
            device_id_type=pl.DeviceIdType.MESH,
        )

    def start(step, carry):
        copy(step).start()
        return carry

    def finish(step, carry):
        copy(step).wait()
        return carry

    lax.fori_loop(1, devices, start, 0)
    own.wait()
    lax.fori_loop(1, devices, finish, 0)


def few_snapshots(snapshots, directions, positions, look_counts, bin_order):
    devices = lax.axis_size("bins")
    block, total_bins, _, sensors = snapshots.shape
    per_device = total_bins // devices
    looks = directions.shape[2]
    by_bin = snapshots.reshape(block, total_bins, 2 * sensors).transpose(1, 0, 2)
    smem = pl.BlockSpec(memory_space=pltpu.SMEM)
    vmem = pl.BlockSpec(memory_space=pltpu.VMEM)
    shape = (devices, per_device * block, 2 * sensors)
    arrived = pl.pallas_call(
        functools.partial(exchange_kernel, devices, per_device),
        out_shape=jax.ShapeDtypeStruct(shape, BF16),
        in_specs=[smem, vmem],
        out_specs=vmem,
        scratch_shapes=[
            pltpu.VMEM(shape, BF16),
            pltpu.SemaphoreType.DMA((devices,)),
            pltpu.SemaphoreType.DMA((devices,)),
            pltpu.SemaphoreType.DMA,
        ],
        compiler_params=pltpu.CompilerParams(
            collective_id=0, has_side_effects=True, vmem_limit_bytes=16 * 1024 * 1024
        ),
    )(bin_order, by_bin)
    arrived = arrived.reshape(devices * per_device * block, 2 * sensors)
    snap = devices * block
    return pl.pallas_call(
        functools.partial(image_kernel, per_device, total_bins),
        out_shape=jax.ShapeDtypeStruct((per_device, looks), F32),
        in_specs=[smem, smem, vmem, vmem, vmem],
        out_specs=vmem,
        scratch_shapes=[
            pltpu.VMEM((per_device, 2, 2 * snap, 2 * sensors), BF16),
            pltpu.VMEM((per_device, 2 * sensors, 2 * snap), BF16),
            pltpu.VMEM((2, sensors, 128), F32),
        ],
        compiler_params=pltpu.CompilerParams(vmem_limit_bytes=40 * 1024 * 1024),
    )(bin_order, look_counts, arrived, directions, positions.T)


def image_bin(stacked, angles, positions, look_count, bin_id, total_bins):
    sensors = positions.shape[1]
    snap_total = stacked.shape[0]
    looks = angles.shape[1]
    products = lax.dot_general(
        stacked, stacked, (((0,), (0,)), ((), ())), preferred_element_type=jnp.float32
    )
    real_cov = (products[:sensors, :sensors] + products[sensors:, sensors:]) / snap_total
    imag_cov = (products[sensors:, :sensors] - products[:sensors, sensors:]) / snap_total
    embedded = jnp.concatenate(
        [jnp.concatenate([real_cov, -imag_cov], 1), jnp.concatenate([imag_cov, real_cov], 1)], 0
    )
    identity = jnp.eye(2 * sensors, dtype=jnp.float32)
    factor = jnp.linalg.cholesky(embedded + 0.1 * identity)
    inverse = lax.linalg.triangular_solve(factor, identity, left_side=True, lower=True)
    freq_ratio = 0.5 + (bin_id.astype(jnp.float32) + 0.5) / total_bins
    active = (look_count + LOOK_BLK - 1) // LOOK_BLK

    def one_block(block, powers):
        offset = block * LOOK_BLK
        piece = lax.dynamic_slice_in_dim(angles, offset, LOOK_BLK, 1)
        phases = (
            2.0
            * math.pi
            * freq_ratio
            * (
                positions[0][:, None] * piece[0][None, :]
                + positions[1][:, None] * piece[1][None, :]
            )
        )
        steering = jnp.concatenate([jnp.cos(phases), -jnp.sin(phases)], 0)
        whitened = jnp.dot(
            inverse, steering, precision=lax.Precision.HIGHEST, preferred_element_type=jnp.float32
        )
        quadratic = jnp.sum(whitened * whitened, 0)
        look_index = offset + jnp.arange(LOOK_BLK, dtype=jnp.int32)
        values = jnp.where(look_index < look_count, sensors / quadratic, jnp.zeros_like(quadratic))
        return lax.dynamic_update_slice_in_dim(powers, values, offset, 0)

    return lax.fori_loop(0, active, one_block, jnp.zeros((looks,), jnp.float32))


def many_snapshots(snapshots, directions, positions, look_counts, bin_order):
    devices = lax.axis_size("bins")
    device = lax.axis_index("bins")
    total_bins = snapshots.shape[1]
    per_device = total_bins // devices
    sensors = snapshots.shape[3]
    bin_ids = device * per_device + jnp.arange(per_device, dtype=jnp.int32)
    turned = lax.all_to_all(snapshots, "bins", split_axis=1, concat_axis=0, tiled=True)
    snap_total = turned.shape[0]
    rows = []
    for local in range(per_device):
        bin_id = bin_ids[local]
        stacked = turned[:, local].reshape(snap_total, 2 * sensors)
        angles = lax.dynamic_index_in_dim(directions, bin_id, 0, keepdims=False)
        look_count = lax.dynamic_index_in_dim(look_counts, bin_id, 0, keepdims=False)
        rows.append(image_bin(stacked, angles, positions, look_count, bin_id, total_bins))
    powers = jnp.stack(rows, 0)
    whole = lax.all_gather(powers, "bins", axis=0, tiled=True)
    my_rows = lax.dynamic_slice_in_dim(bin_order, device * per_device, per_device)
    powers = jnp.take(whole, my_rows, axis=0)
    return powers


def body(snapshots, directions, positions, look_counts, bin_order):
    snap_total = snapshots.shape[0] * lax.axis_size("bins")
    form = few_snapshots if snap_total < snapshots.shape[3] else many_snapshots
    return form(snapshots, directions, positions, look_counts, bin_order)


def solution(mesh):
    placed = (
        P(("groups", "bins"), None, None, None),
        P("groups", None, None),
        P(),
        P("groups"),
        P("groups"),
    )
    return jax.shard_map(
        body, mesh=mesh, in_specs=placed, out_specs=P(("groups", "bins"), None), check_vma=False
    )
```

```python
import functools
import math

import jax
import jax.numpy as jnp
from jax import lax
from jax.experimental import pallas as pl
from jax.experimental.pallas import tpu as pltpu
from jax.sharding import PartitionSpec as P

LOOK_BLK = 128
LOADING = 0.1
PIVOT = 32
WIDE = 512
COS_TERMS = (6.528658390045166, -25.967599868774414, 60.16762924194336, -85.45014190673828,
             64.93911743164062, -19.73920440673828, 1.0)
SIN_TERMS = (3.2381374835968018, -14.899847030639648, 42.02592849731445, -76.70301818847656,
             81.60513305664062, -41.34170150756836, 6.2831854820251465)
F32 = jnp.float32
BF16 = jnp.bfloat16


def mm(a, b, dims=((1,), (0,)), exact=False):
    precision = lax.Precision.HIGHEST if exact else None
    return lax.dot_general(a, b, (dims, ((), ())), precision=precision, preferred_element_type=F32)


def halves(x):
    high = x.astype(BF16)
    return high, (x - high.astype(F32)).astype(BF16)


def polynomial(z, terms):
    value = z * terms[0] + terms[1]
    for term in terms[2:]:
        value = value * z + term
    return value


def invert_small(blocks):
    n = blocks[0][0].shape[0]
    rows = lax.broadcasted_iota(jnp.int32, (n, n), 0)
    cols = lax.broadcasted_iota(jnp.int32, (n, n), 1)
    one_row = lax.broadcasted_iota(jnp.int32, (1, n), 1)
    blocks = list(blocks)
    for k in range(n):
        for i, (re, im) in enumerate(blocks):
            col_re = jnp.broadcast_to(re[:, k : k + 1], (n, n))
            col_im = jnp.broadcast_to(im[:, k : k + 1], (n, n))
            scale = 1.0 / col_re[k : k + 1, :]
            row_re = jnp.where(one_row == k, 1.0, re[k : k + 1, :]) * scale
            row_im = jnp.where(one_row == k, 0.0, im[k : k + 1, :]) * scale
            rest_re = jnp.where(cols == k, 0.0, re)
            rest_im = jnp.where(cols == k, 0.0, im)
            next_re = rest_re - col_re * row_re + col_im * row_im
            next_im = rest_im - col_re * row_im - col_im * row_re
            blocks[i] = (
                jnp.where(rows == k, row_re, next_re),
                jnp.where(rows == k, row_im, next_im),
            )
    return blocks


def put_rows(whole, rows, start):
    stop = start + rows.shape[0]
    pieces = [rows]
    if start:
        pieces.insert(0, whole[:start])
    if stop < whole.shape[0]:
        pieces.append(whole[stop:])
    return jnp.concatenate(pieces, 0)


def invert(mats):
    n = mats[0][0].shape[0]
    mats = list(mats)
    for start in range(0, n, PIVOT):
        stop = start + PIVOT
        small = invert_small([(re[start:stop, start:stop], im[start:stop, start:stop]) for re, im in mats])
        cols = lax.broadcasted_iota(jnp.int32, (n, n), 1)
        inside = (cols >= start) & (cols < stop)
        unit = lax.broadcasted_iota(jnp.int32, (PIVOT, n), 0) + start == lax.broadcasted_iota(
            jnp.int32, (PIVOT, n), 1
        )
        band = inside[:PIVOT]
        for i, (re, im) in enumerate(mats):
            row_re = jnp.where(band, unit.astype(F32), re[start:stop])
            row_im = jnp.where(band, 0.0, im[start:stop])
            d_re, d_im = small[i]
            both = jnp.concatenate([row_re, row_im], 1)
            p = mm(d_re, both, exact=True)
            q = mm(d_im, both, exact=True)
            t_re = p[:, :n] - q[:, n:]
            t_im = p[:, n:] + q[:, :n]
            both = jnp.concatenate([t_re, t_im], 1)
            p = mm(re[:, start:stop], both, exact=True)
            q = mm(im[:, start:stop], both, exact=True)
            next_re = jnp.where(inside, 0.0, re) - p[:, :n] + q[:, n:]
            next_im = jnp.where(inside, 0.0, im) - p[:, n:] - q[:, :n]
            mats[i] = (put_rows(next_re, t_re, start), put_rows(next_im, t_im, start))
    return mats


def image_kernel(per_device, total_bins, order_ref, counts_ref, snaps_ref, directions_ref, spots_ref, out_ref,
                 solver_ref, turned_ref, spot_ref):
    first = lax.axis_index("bins") * per_device
    snap = snaps_ref.shape[0] // per_device
    sensors = spots_ref.shape[0]
    looks = out_ref.shape[1]
    ridge = LOADING * snap
    both = snaps_ref[...].astype(F32).reshape(snap // 8, per_device, 8, 2 * sensors)
    diag = lax.broadcasted_iota(jnp.int32, (snap, snap), 0) == lax.broadcasted_iota(jnp.int32, (snap, snap), 1)
    mats, fields = [], []
    for local in range(per_device):
        data = both[:, local].reshape(snap, 2 * sensors)
        turned = jnp.concatenate([-data[:, sensors:], data[:, :sensors]], 1)
        top, low = data.astype(BF16), turned.astype(BF16)
        gram_re = mm(top, top, ((1,), (1,)))
        gram_im = mm(low, top, ((1,), (1,)))
        mats.append((gram_re + jnp.where(diag, ridge, 0.0), gram_im))
        fields.append((top, low))
        turned_ref[local] = jnp.concatenate([data, turned], 0).T.astype(BF16)
    mats = invert(mats)
    for local in range(per_device):
        re, im = mats[local]
        stacked = jnp.concatenate(fields[local], 0)
        high, low = halves(jnp.concatenate([re, -im], 1))
        upper = mm(high, stacked) + mm(low, stacked)
        lower = jnp.concatenate([-upper[:, sensors:], upper[:, :sensors]], 1)
        high, low = halves(jnp.concatenate([upper, lower], 0))
        solver_ref[local, 0] = high
        solver_ref[local, 1] = low
    out_ref[...] = jnp.zeros_like(out_ref)
    for local in range(per_device):
        bin_id = order_ref[first + local]
        count = counts_ref[bin_id]
        ratio = 0.5 + (bin_id.astype(F32) + 0.5) / total_bins
        spot_ref[0] = jnp.broadcast_to(spots_ref[:, 0:1] * ratio, (sensors, 128))
        spot_ref[1] = jnp.broadcast_to(spots_ref[:, 1:2] * ratio, (sensors, 128))

        def one_block(block, carry):
            offset = pl.multiple_of(block * WIDE, WIDE)
            piece = directions_ref[bin_id, :, pl.ds(offset, WIDE)]
            x = jnp.concatenate([spot_ref[0]] * (WIDE // 128), 1)
            y = jnp.concatenate([spot_ref[1]] * (WIDE // 128), 1)
            turns = x * piece[0:1] + y * piece[1:2]
            turns = turns - jnp.round(turns)
            z = turns * turns
            cosine = polynomial(z, COS_TERMS)
            sine = polynomial(z, SIN_TERMS) * turns
            steering = jnp.concatenate([cosine, -sine], 0)
            s_high, s_low = halves(steering)
            weights = mm(solver_ref[local, 0], s_high) + mm(solver_ref[local, 1], s_high) + mm(solver_ref[local, 0], s_low)
            w_high, w_low = halves(weights)
            fitted = mm(turned_ref[local], w_high) + mm(turned_ref[local], w_low)
            left = steering - fitted
            power = jnp.sum(left * left, 0, keepdims=True) + ridge * jnp.sum(weights * weights, 0, keepdims=True)
            index = offset + lax.broadcasted_iota(jnp.int32, (1, WIDE), 1)
            out_ref[local : local + 1, pl.ds(offset, WIDE)] = jnp.where(index < count, LOADING * sensors / power, 0.0)
            return carry

        lax.fori_loop(0, (count + WIDE - 1) // WIDE, one_block, 0)


def exchange_kernel(devices, per_device, order_ref, snaps_ref, out_ref, send_ref, send_sem, recv_sem, own_sem):
    me = lax.axis_index("bins")
    barrier = pltpu.get_barrier_semaphore()

    def greet(step, carry):
        peer = lax.rem(me + step, devices)
        pl.semaphore_signal(barrier, inc=1, device_id={"bins": peer}, device_id_type=pl.DeviceIdType.MESH)
        return carry

    lax.fori_loop(1, devices, greet, 0)
    for owner in range(devices):
        pieces = [snaps_ref[order_ref[owner * per_device + local]].astype(F32) for local in range(per_device)]
        send_ref[owner] = jnp.concatenate(pieces, 0).astype(BF16)
    own = pltpu.make_async_copy(send_ref.at[me], out_ref.at[me], own_sem)
    own.start()
    pl.semaphore_wait(barrier, devices - 1)

    def copy(step):
        peer = lax.rem(me + step, devices)
        return pltpu.make_async_remote_copy(
            src_ref=send_ref.at[peer],
            dst_ref=out_ref.at[me],
            send_sem=send_sem.at[step],
            recv_sem=recv_sem.at[step],
            device_id={"bins": peer},
            device_id_type=pl.DeviceIdType.MESH,
        )

    def start(step, carry):
        copy(step).start()
        return carry

    def finish(step, carry):
        copy(step).wait()
        return carry

    lax.fori_loop(1, devices, start, 0)
    own.wait()
    lax.fori_loop(1, devices, finish, 0)


def few_snapshots(snapshots, directions, positions, look_counts, bin_order):
    devices = lax.axis_size("bins")
    block, total_bins, _, sensors = snapshots.shape
    per_device = total_bins // devices
    looks = directions.shape[2]
    by_bin = snapshots.reshape(block, total_bins, 2 * sensors).transpose(1, 0, 2)
    smem = pl.BlockSpec(memory_space=pltpu.SMEM)
    vmem = pl.BlockSpec(memory_space=pltpu.VMEM)
    shape = (devices, per_device * block, 2 * sensors)
    arrived = pl.pallas_call(
        functools.partial(exchange_kernel, devices, per_device),
        out_shape=jax.ShapeDtypeStruct(shape, BF16),
        in_specs=[smem, vmem],
        out_specs=vmem,
        scratch_shapes=[
            pltpu.VMEM(shape, BF16),
            pltpu.SemaphoreType.DMA((devices,)),
            pltpu.SemaphoreType.DMA((devices,)),
            pltpu.SemaphoreType.DMA,
        ],
        compiler_params=pltpu.CompilerParams(
            collective_id=0, has_side_effects=True, vmem_limit_bytes=16 * 1024 * 1024
        ),
    )(bin_order, by_bin)
    arrived = arrived.reshape(devices * per_device * block, 2 * sensors)
    snap = devices * block
    return pl.pallas_call(
        functools.partial(image_kernel, per_device, total_bins),
        out_shape=jax.ShapeDtypeStruct((per_device, looks), F32),
        in_specs=[smem, smem, vmem, vmem, vmem],
        out_specs=vmem,
        scratch_shapes=[
            pltpu.VMEM((per_device, 2, 2 * snap, 2 * sensors), BF16),
            pltpu.VMEM((per_device, 2 * sensors, 2 * snap), BF16),
            pltpu.VMEM((2, sensors, 128), F32),
        ],
        compiler_params=pltpu.CompilerParams(vmem_limit_bytes=40 * 1024 * 1024),
    )(bin_order, look_counts, arrived, directions, positions.T)


def image_bin(stacked, angles, positions, look_count, bin_id, total_bins):
    sensors = positions.shape[1]
    snap_total = stacked.shape[0]
    looks = angles.shape[1]
    products = lax.dot_general(
        stacked, stacked, (((0,), (0,)), ((), ())), preferred_element_type=jnp.float32
    )
    real_cov = (products[:sensors, :sensors] + products[sensors:, sensors:]) / snap_total
    imag_cov = (products[sensors:, :sensors] - products[:sensors, sensors:]) / snap_total
    embedded = jnp.concatenate(
        [jnp.concatenate([real_cov, -imag_cov], 1), jnp.concatenate([imag_cov, real_cov], 1)], 0
    )
    identity = jnp.eye(2 * sensors, dtype=jnp.float32)
    factor = jnp.linalg.cholesky(embedded + 0.1 * identity)
    inverse = lax.linalg.triangular_solve(factor, identity, left_side=True, lower=True)
    freq_ratio = 0.5 + (bin_id.astype(jnp.float32) + 0.5) / total_bins
    active = (look_count + LOOK_BLK - 1) // LOOK_BLK

    def one_block(block, powers):
        offset = block * LOOK_BLK
        piece = lax.dynamic_slice_in_dim(angles, offset, LOOK_BLK, 1)
        phases = (
            2.0
            * math.pi
            * freq_ratio
            * (
                positions[0][:, None] * piece[0][None, :]
                + positions[1][:, None] * piece[1][None, :]
            )
        )
        steering = jnp.concatenate([jnp.cos(phases), -jnp.sin(phases)], 0)
        whitened = jnp.dot(
            inverse, steering, precision=lax.Precision.HIGHEST, preferred_element_type=jnp.float32
        )
        quadratic = jnp.sum(whitened * whitened, 0)
        look_index = offset + jnp.arange(LOOK_BLK, dtype=jnp.int32)
        values = jnp.where(look_index < look_count, sensors / quadratic, jnp.zeros_like(quadratic))
        return lax.dynamic_update_slice_in_dim(powers, values, offset, 0)

    return lax.fori_loop(0, active, one_block, jnp.zeros((looks,), jnp.float32))


def many_snapshots(snapshots, directions, positions, look_counts, bin_order):
    devices = lax.axis_size("bins")
    device = lax.axis_index("bins")
    total_bins = snapshots.shape[1]
    per_device = total_bins // devices
    sensors = snapshots.shape[3]
    bin_ids = device * per_device + jnp.arange(per_device, dtype=jnp.int32)
    turned = lax.all_to_all(snapshots, "bins", split_axis=1, concat_axis=0, tiled=True)
    snap_total = turned.shape[0]
    rows = []
    for local in range(per_device):
        bin_id = bin_ids[local]
        stacked = turned[:, local].reshape(snap_total, 2 * sensors)
        angles = lax.dynamic_index_in_dim(directions, bin_id, 0, keepdims=False)
        look_count = lax.dynamic_index_in_dim(look_counts, bin_id, 0, keepdims=False)
        rows.append(image_bin(stacked, angles, positions, look_count, bin_id, total_bins))
    powers = jnp.stack(rows, 0)
    whole = lax.all_gather(powers, "bins", axis=0, tiled=True)
    my_rows = lax.dynamic_slice_in_dim(bin_order, device * per_device, per_device)
    powers = jnp.take(whole, my_rows, axis=0)
    return powers


def body(snapshots, directions, positions, look_counts, bin_order):
    snap_total = snapshots.shape[0] * lax.axis_size("bins")
    form = few_snapshots if snap_total < snapshots.shape[3] else many_snapshots
    return form(snapshots, directions, positions, look_counts, bin_order)


def solution(mesh):
    placed = (
        P(("groups", "bins"), None, None, None),
        P("groups", None, None),
        P(),
        P("groups"),
        P("groups"),
    )
    return jax.shard_map(
        body, mesh=mesh, in_specs=placed, out_specs=P(("groups", "bins"), None), check_vma=False
    )
```

```python
import functools
import math

import jax
import jax.numpy as jnp
from jax import lax
from jax.experimental import pallas as pl
from jax.experimental.pallas import tpu as pltpu
from jax.sharding import PartitionSpec as P

LOOK_BLK = 128
LOADING = 0.1
PIVOT = 64
WIDE = 512
COS_TERMS = (6.528658390045166, -25.967599868774414, 60.16762924194336, -85.45014190673828,
             64.93911743164062, -19.73920440673828, 1.0)
SIN_TERMS = (3.2381374835968018, -14.899847030639648, 42.02592849731445, -76.70301818847656,
             81.60513305664062, -41.34170150756836, 6.2831854820251465)
F32 = jnp.float32
BF16 = jnp.bfloat16


def mm(a, b, dims=((1,), (0,)), exact=False):
    precision = lax.Precision.HIGHEST if exact else None
    return lax.dot_general(a, b, (dims, ((), ())), precision=precision, preferred_element_type=F32)


def halves(x):
    high = x.astype(BF16)
    return high, (x - high.astype(F32)).astype(BF16)


def polynomial(z, terms):
    value = z * terms[0] + terms[1]
    for term in terms[2:]:
        value = value * z + term
    return value


def invert_small(blocks):
    n = blocks[0][0].shape[0]
    rows = lax.broadcasted_iota(jnp.int32, (n, n), 0)
    cols = lax.broadcasted_iota(jnp.int32, (n, n), 1)
    one_row = lax.broadcasted_iota(jnp.int32, (1, n), 1)
    blocks = list(blocks)
    for k in range(n):
        for i, (re, im) in enumerate(blocks):
            col_re = jnp.broadcast_to(re[:, k : k + 1], (n, n))
            col_im = jnp.broadcast_to(im[:, k : k + 1], (n, n))
            scale = 1.0 / col_re[k : k + 1, :]
            row_re = jnp.where(one_row == k, 1.0, re[k : k + 1, :]) * scale
            row_im = jnp.where(one_row == k, 0.0, im[k : k + 1, :]) * scale
            rest_re = jnp.where(cols == k, 0.0, re)
            rest_im = jnp.where(cols == k, 0.0, im)
            next_re = rest_re - col_re * row_re + col_im * row_im
            next_im = rest_im - col_re * row_im - col_im * row_re
            blocks[i] = (
                jnp.where(rows == k, row_re, next_re),
                jnp.where(rows == k, row_im, next_im),
            )
    return blocks


def put_rows(whole, rows, start):
    stop = start + rows.shape[0]
    pieces = [rows]
    if start:
        pieces.insert(0, whole[:start])
    if stop < whole.shape[0]:
        pieces.append(whole[stop:])
    return jnp.concatenate(pieces, 0)


def invert(mats):
    n = mats[0][0].shape[0]
    mats = list(mats)
    for start in range(0, n, PIVOT):
        stop = start + PIVOT
        small = invert_small([(re[start:stop, start:stop], im[start:stop, start:stop]) for re, im in mats])
        cols = lax.broadcasted_iota(jnp.int32, (n, n), 1)
        inside = (cols >= start) & (cols < stop)
        unit = lax.broadcasted_iota(jnp.int32, (PIVOT, n), 0) + start == lax.broadcasted_iota(
            jnp.int32, (PIVOT, n), 1
        )
        band = inside[:PIVOT]
        for i, (re, im) in enumerate(mats):
            row_re = jnp.where(band, unit.astype(F32), re[start:stop])
            row_im = jnp.where(band, 0.0, im[start:stop])
            d_re, d_im = small[i]
            both = jnp.concatenate([row_re, row_im], 1)
            p = mm(d_re, both, exact=True)
            q = mm(d_im, both, exact=True)
            t_re = p[:, :n] - q[:, n:]
            t_im = p[:, n:] + q[:, :n]
            both = jnp.concatenate([t_re, t_im], 1)
            p = mm(re[:, start:stop], both, exact=True)
            q = mm(im[:, start:stop], both, exact=True)
            next_re = jnp.where(inside, 0.0, re) - p[:, :n] + q[:, n:]
            next_im = jnp.where(inside, 0.0, im) - p[:, n:] - q[:, :n]
            mats[i] = (put_rows(next_re, t_re, start), put_rows(next_im, t_im, start))
    return mats


def image_kernel(per_device, total_bins, order_ref, counts_ref, snaps_ref, directions_ref, spots_ref, out_ref,
                 solver_ref, turned_ref, spot_ref):
    first = lax.axis_index("bins") * per_device
    snap = snaps_ref.shape[0] // per_device
    sensors = spots_ref.shape[0]
    looks = out_ref.shape[1]
    ridge = LOADING * snap
    both = snaps_ref[...].astype(F32).reshape(snap // 8, per_device, 8, 2 * sensors)
    diag = lax.broadcasted_iota(jnp.int32, (snap, snap), 0) == lax.broadcasted_iota(jnp.int32, (snap, snap), 1)
    mats, fields = [], []
    for local in range(per_device):
        data = both[:, local].reshape(snap, 2 * sensors)
        turned = jnp.concatenate([-data[:, sensors:], data[:, :sensors]], 1)
        top, low = data.astype(BF16), turned.astype(BF16)
        gram_re = mm(top, top, ((1,), (1,)))
        gram_im = mm(low, top, ((1,), (1,)))
        mats.append((gram_re + jnp.where(diag, ridge, 0.0), gram_im))
        fields.append((top, low))
        turned_ref[local] = jnp.concatenate([data, turned], 0).T.astype(BF16)
    mats = invert(mats)
    for local in range(per_device):
        re, im = mats[local]
        stacked = jnp.concatenate(fields[local], 0)
        high, low = halves(jnp.concatenate([re, -im], 1))
        upper = mm(high, stacked) + mm(low, stacked)
        lower = jnp.concatenate([-upper[:, sensors:], upper[:, :sensors]], 1)
        high, low = halves(jnp.concatenate([upper, lower], 0))
        solver_ref[local, 0] = high
        solver_ref[local, 1] = low
    out_ref[...] = jnp.zeros_like(out_ref)
    for local in range(per_device):
        bin_id = order_ref[first + local]
        count = counts_ref[bin_id]
        ratio = 0.5 + (bin_id.astype(F32) + 0.5) / total_bins
        spot_ref[0] = jnp.broadcast_to(spots_ref[:, 0:1] * ratio, (sensors, 128))
        spot_ref[1] = jnp.broadcast_to(spots_ref[:, 1:2] * ratio, (sensors, 128))

        def one_block(block, carry):
            offset = pl.multiple_of(block * WIDE, WIDE)
            piece = directions_ref[bin_id, :, pl.ds(offset, WIDE)]
            x = jnp.concatenate([spot_ref[0]] * (WIDE // 128), 1)
            y = jnp.concatenate([spot_ref[1]] * (WIDE // 128), 1)
            turns = x * piece[0:1] + y * piece[1:2]
            turns = turns - jnp.round(turns)
            z = turns * turns
            cosine = polynomial(z, COS_TERMS)
            sine = polynomial(z, SIN_TERMS) * turns
            steering = jnp.concatenate([cosine, -sine], 0)
            s_high, s_low = halves(steering)
            weights = mm(solver_ref[local, 0], s_high) + mm(solver_ref[local, 1], s_high) + mm(solver_ref[local, 0], s_low)
            w_high, w_low = halves(weights)
            fitted = mm(turned_ref[local], w_high) + mm(turned_ref[local], w_low)
            left = steering - fitted
            power = jnp.sum(left * left, 0, keepdims=True) + ridge * jnp.sum(weights * weights, 0, keepdims=True)
            index = offset + lax.broadcasted_iota(jnp.int32, (1, WIDE), 1)
            out_ref[local : local + 1, pl.ds(offset, WIDE)] = jnp.where(index < count, LOADING * sensors / power, 0.0)
            return carry

        lax.fori_loop(0, (count + WIDE - 1) // WIDE, one_block, 0)


def exchange_kernel(devices, per_device, order_ref, snaps_ref, out_ref, send_ref, send_sem, recv_sem, own_sem):
    me = lax.axis_index("bins")
    barrier = pltpu.get_barrier_semaphore()

    def greet(step, carry):
        peer = lax.rem(me + step, devices)
        pl.semaphore_signal(barrier, inc=1, device_id={"bins": peer}, device_id_type=pl.DeviceIdType.MESH)
        return carry

    lax.fori_loop(1, devices, greet, 0)
    for owner in range(devices):
        pieces = [snaps_ref[order_ref[owner * per_device + local]].astype(F32) for local in range(per_device)]
        send_ref[owner] = jnp.concatenate(pieces, 0).astype(BF16)
    own = pltpu.make_async_copy(send_ref.at[me], out_ref.at[me], own_sem)
    own.start()
    pl.semaphore_wait(barrier, devices - 1)

    def copy(step):
        peer = lax.rem(me + step, devices)
        return pltpu.make_async_remote_copy(
            src_ref=send_ref.at[peer],
            dst_ref=out_ref.at[me],
            send_sem=send_sem.at[step],
            recv_sem=recv_sem.at[step],
            device_id={"bins": peer},
            device_id_type=pl.DeviceIdType.MESH,
        )

    def start(step, carry):
        copy(step).start()
        return carry

    def finish(step, carry):
        copy(step).wait()
        return carry

    lax.fori_loop(1, devices, start, 0)
    own.wait()
    lax.fori_loop(1, devices, finish, 0)


def few_snapshots(snapshots, directions, positions, look_counts, bin_order):
    devices = lax.axis_size("bins")
    block, total_bins, _, sensors = snapshots.shape
    per_device = total_bins // devices
    looks = directions.shape[2]
    by_bin = snapshots.reshape(block, total_bins, 2 * sensors).transpose(1, 0, 2)
    smem = pl.BlockSpec(memory_space=pltpu.SMEM)
    vmem = pl.BlockSpec(memory_space=pltpu.VMEM)
    shape = (devices, per_device * block, 2 * sensors)
    arrived = pl.pallas_call(
        functools.partial(exchange_kernel, devices, per_device),
        out_shape=jax.ShapeDtypeStruct(shape, BF16),
        in_specs=[smem, vmem],
        out_specs=vmem,
        scratch_shapes=[
            pltpu.VMEM(shape, BF16),
            pltpu.SemaphoreType.DMA((devices,)),
            pltpu.SemaphoreType.DMA((devices,)),
            pltpu.SemaphoreType.DMA,
        ],
        compiler_params=pltpu.CompilerParams(
            collective_id=0, has_side_effects=True, vmem_limit_bytes=16 * 1024 * 1024
        ),
    )(bin_order, by_bin)
    arrived = arrived.reshape(devices * per_device * block, 2 * sensors)
    snap = devices * block
    return pl.pallas_call(
        functools.partial(image_kernel, per_device, total_bins),
        out_shape=jax.ShapeDtypeStruct((per_device, looks), F32),
        in_specs=[smem, smem, vmem, vmem, vmem],
        out_specs=vmem,
        scratch_shapes=[
            pltpu.VMEM((per_device, 2, 2 * snap, 2 * sensors), BF16),
            pltpu.VMEM((per_device, 2 * sensors, 2 * snap), BF16),
            pltpu.VMEM((2, sensors, 128), F32),
        ],
        compiler_params=pltpu.CompilerParams(vmem_limit_bytes=40 * 1024 * 1024),
    )(bin_order, look_counts, arrived, directions, positions.T)


def image_bin(stacked, angles, positions, look_count, bin_id, total_bins):
    sensors = positions.shape[1]
    snap_total = stacked.shape[0]
    looks = angles.shape[1]
    products = lax.dot_general(
        stacked, stacked, (((0,), (0,)), ((), ())), preferred_element_type=jnp.float32
    )
    real_cov = (products[:sensors, :sensors] + products[sensors:, sensors:]) / snap_total
    imag_cov = (products[sensors:, :sensors] - products[:sensors, sensors:]) / snap_total
    embedded = jnp.concatenate(
        [jnp.concatenate([real_cov, -imag_cov], 1), jnp.concatenate([imag_cov, real_cov], 1)], 0
    )
    identity = jnp.eye(2 * sensors, dtype=jnp.float32)
    factor = jnp.linalg.cholesky(embedded + 0.1 * identity)
    inverse = lax.linalg.triangular_solve(factor, identity, left_side=True, lower=True)
    freq_ratio = 0.5 + (bin_id.astype(jnp.float32) + 0.5) / total_bins
    active = (look_count + LOOK_BLK - 1) // LOOK_BLK

    def one_block(block, powers):
        offset = block * LOOK_BLK
        piece = lax.dynamic_slice_in_dim(angles, offset, LOOK_BLK, 1)
        phases = (
            2.0
            * math.pi
            * freq_ratio
            * (
                positions[0][:, None] * piece[0][None, :]
                + positions[1][:, None] * piece[1][None, :]
            )
        )
        steering = jnp.concatenate([jnp.cos(phases), -jnp.sin(phases)], 0)
        whitened = jnp.dot(
            inverse, steering, precision=lax.Precision.HIGHEST, preferred_element_type=jnp.float32
        )
        quadratic = jnp.sum(whitened * whitened, 0)
        look_index = offset + jnp.arange(LOOK_BLK, dtype=jnp.int32)
        values = jnp.where(look_index < look_count, sensors / quadratic, jnp.zeros_like(quadratic))
        return lax.dynamic_update_slice_in_dim(powers, values, offset, 0)

    return lax.fori_loop(0, active, one_block, jnp.zeros((looks,), jnp.float32))


def many_snapshots(snapshots, directions, positions, look_counts, bin_order):
    devices = lax.axis_size("bins")
    device = lax.axis_index("bins")
    total_bins = snapshots.shape[1]
    per_device = total_bins // devices
    sensors = snapshots.shape[3]
    bin_ids = device * per_device + jnp.arange(per_device, dtype=jnp.int32)
    turned = lax.all_to_all(snapshots, "bins", split_axis=1, concat_axis=0, tiled=True)
    snap_total = turned.shape[0]
    rows = []
    for local in range(per_device):
        bin_id = bin_ids[local]
        stacked = turned[:, local].reshape(snap_total, 2 * sensors)
        angles = lax.dynamic_index_in_dim(directions, bin_id, 0, keepdims=False)
        look_count = lax.dynamic_index_in_dim(look_counts, bin_id, 0, keepdims=False)
        rows.append(image_bin(stacked, angles, positions, look_count, bin_id, total_bins))
    powers = jnp.stack(rows, 0)
    whole = lax.all_gather(powers, "bins", axis=0, tiled=True)
    my_rows = lax.dynamic_slice_in_dim(bin_order, device * per_device, per_device)
    powers = jnp.take(whole, my_rows, axis=0)
    return powers


def body(snapshots, directions, positions, look_counts, bin_order):
    snap_total = snapshots.shape[0] * lax.axis_size("bins")
    form = few_snapshots if snap_total < snapshots.shape[3] else many_snapshots
    return form(snapshots, directions, positions, look_counts, bin_order)


def solution(mesh):
    placed = (
        P(("groups", "bins"), None, None, None),
        P("groups", None, None),
        P(),
        P("groups"),
        P("groups"),
    )
    return jax.shard_map(
        body, mesh=mesh, in_specs=placed, out_specs=P(("groups", "bins"), None), check_vma=False
    )
```

```python
import functools
import math

import jax
import jax.numpy as jnp
from jax import lax
from jax.experimental import pallas as pl
from jax.experimental.pallas import tpu as pltpu
from jax.sharding import PartitionSpec as P

LOOK_BLK = 128
LOADING = 0.1
PIVOT = 64
WIDE = 512
COS_TERMS = (6.528658390045166, -25.967599868774414, 60.16762924194336, -85.45014190673828,
             64.93911743164062, -19.73920440673828, 1.0)
SIN_TERMS = (3.2381374835968018, -14.899847030639648, 42.02592849731445, -76.70301818847656,
             81.60513305664062, -41.34170150756836, 6.2831854820251465)
F32 = jnp.float32
BF16 = jnp.bfloat16


def mm(a, b, dims=((1,), (0,)), exact=False):
    precision = lax.Precision.HIGHEST if exact else None
    return lax.dot_general(a, b, (dims, ((), ())), precision=precision, preferred_element_type=F32)


def halves(x):
    high = x.astype(BF16)
    return high, (x - high.astype(F32)).astype(BF16)


def polynomial(z, terms):
    value = z * terms[0] + terms[1]
    for term in terms[2:]:
        value = value * z + term
    return value


def invert_small(blocks):
    n = blocks[0][0].shape[0]
    rows = lax.broadcasted_iota(jnp.int32, (n, n), 0)
    cols = lax.broadcasted_iota(jnp.int32, (n, n), 1)
    one_row = lax.broadcasted_iota(jnp.int32, (1, n), 1)
    blocks = list(blocks)
    for k in range(0, n, 2):
        pair = (cols == k) | (cols == k + 1)
        for i, (re, im) in enumerate(blocks):
            c0_re = jnp.broadcast_to(re[:, k : k + 1], (n, n))
            c0_im = jnp.broadcast_to(im[:, k : k + 1], (n, n))
            c1_re = jnp.broadcast_to(re[:, k + 1 : k + 2], (n, n))
            c1_im = jnp.broadcast_to(im[:, k + 1 : k + 2], (n, n))
            a, c = c0_re[k : k + 1], c1_re[k + 1 : k + 2]
            b_re, b_im = c1_re[k : k + 1], c1_im[k : k + 1]
            scale = 1.0 / (a * c - (b_re * b_re + b_im * b_im))
            a, c, b_re, b_im = a * scale, c * scale, b_re * scale, b_im * scale
            edge = (one_row == k) | (one_row == k + 1)
            r0_re = jnp.where(edge, jnp.where(one_row == k, 1.0, 0.0), re[k : k + 1])
            r1_re = jnp.where(edge, jnp.where(one_row == k, 0.0, 1.0), re[k + 1 : k + 2])
            r0_im = jnp.where(edge, 0.0, im[k : k + 1])
            r1_im = jnp.where(edge, 0.0, im[k + 1 : k + 2])
            t0_re = c * r0_re - (b_re * r1_re - b_im * r1_im)
            t0_im = c * r0_im - (b_re * r1_im + b_im * r1_re)
            t1_re = a * r1_re - (b_re * r0_re + b_im * r0_im)
            t1_im = a * r1_im - (b_re * r0_im - b_im * r0_re)
            next_re = jnp.where(pair, 0.0, re) - (c0_re * t0_re - c0_im * t0_im) - (c1_re * t1_re - c1_im * t1_im)
            next_im = jnp.where(pair, 0.0, im) - (c0_re * t0_im + c0_im * t0_re) - (c1_re * t1_im + c1_im * t1_re)
            blocks[i] = (
                jnp.where(rows == k, t0_re, jnp.where(rows == k + 1, t1_re, next_re)),
                jnp.where(rows == k, t0_im, jnp.where(rows == k + 1, t1_im, next_im)),
            )
    return blocks


def put_rows(whole, rows, start):
    stop = start + rows.shape[0]
    pieces = [rows]
    if start:
        pieces.insert(0, whole[:start])
    if stop < whole.shape[0]:
        pieces.append(whole[stop:])
    return jnp.concatenate(pieces, 0)


def invert(mats):
    n = mats[0][0].shape[0]
    mats = list(mats)
    for start in range(0, n, PIVOT):
        stop = start + PIVOT
        small = invert_small([(re[start:stop, start:stop], im[start:stop, start:stop]) for re, im in mats])
        cols = lax.broadcasted_iota(jnp.int32, (n, n), 1)
        inside = (cols >= start) & (cols < stop)
        unit = lax.broadcasted_iota(jnp.int32, (PIVOT, n), 0) + start == lax.broadcasted_iota(
            jnp.int32, (PIVOT, n), 1
        )
        band = inside[:PIVOT]
        for i, (re, im) in enumerate(mats):
            row_re = jnp.where(band, unit.astype(F32), re[start:stop])
            row_im = jnp.where(band, 0.0, im[start:stop])
            d_re, d_im = small[i]
            both = jnp.concatenate([row_re, row_im], 1)
            p = mm(d_re, both, exact=True)
            q = mm(d_im, both, exact=True)
            t_re = p[:, :n] - q[:, n:]
            t_im = p[:, n:] + q[:, :n]
            both = jnp.concatenate([t_re, t_im], 1)
            p = mm(re[:, start:stop], both, exact=True)
            q = mm(im[:, start:stop], both, exact=True)
            next_re = jnp.where(inside, 0.0, re) - p[:, :n] + q[:, n:]
            next_im = jnp.where(inside, 0.0, im) - p[:, n:] - q[:, :n]
            mats[i] = (put_rows(next_re, t_re, start), put_rows(next_im, t_im, start))
    return mats


def image_kernel(per_device, total_bins, order_ref, counts_ref, snaps_ref, directions_ref, spots_ref, out_ref,
                 solver_ref, turned_ref, spot_ref):
    first = lax.axis_index("bins") * per_device
    snap = snaps_ref.shape[0] // per_device
    sensors = spots_ref.shape[0]
    looks = out_ref.shape[1]
    ridge = LOADING * snap
    both = snaps_ref[...].astype(F32).reshape(snap // 8, per_device, 8, 2 * sensors)
    diag = lax.broadcasted_iota(jnp.int32, (snap, snap), 0) == lax.broadcasted_iota(jnp.int32, (snap, snap), 1)
    mats, fields = [], []
    for local in range(per_device):
        data = both[:, local].reshape(snap, 2 * sensors)
        turned = jnp.concatenate([-data[:, sensors:], data[:, :sensors]], 1)
        top, low = data.astype(BF16), turned.astype(BF16)
        gram_re = mm(top, top, ((1,), (1,)))
        gram_im = mm(low, top, ((1,), (1,)))
        mats.append((gram_re + jnp.where(diag, ridge, 0.0), gram_im))
        fields.append((top, low))
        turned_ref[local] = jnp.concatenate([data, turned], 0).T.astype(BF16)
    mats = invert(mats)
    for local in range(per_device):
        re, im = mats[local]
        stacked = jnp.concatenate(fields[local], 0)
        high, low = halves(jnp.concatenate([re, -im], 1))
        upper = mm(high, stacked) + mm(low, stacked)
        lower = jnp.concatenate([-upper[:, sensors:], upper[:, :sensors]], 1)
        high, low = halves(jnp.concatenate([upper, lower], 0))
        solver_ref[local, 0] = high
        solver_ref[local, 1] = low
    out_ref[...] = jnp.zeros_like(out_ref)
    for local in range(per_device):
        bin_id = order_ref[first + local]
        count = counts_ref[bin_id]
        ratio = 0.5 + (bin_id.astype(F32) + 0.5) / total_bins
        spot_ref[0] = jnp.broadcast_to(spots_ref[:, 0:1] * ratio, (sensors, 128))
        spot_ref[1] = jnp.broadcast_to(spots_ref[:, 1:2] * ratio, (sensors, 128))

        def one_block(block, carry):
            offset = pl.multiple_of(block * WIDE, WIDE)
            piece = directions_ref[bin_id, :, pl.ds(offset, WIDE)]
            x = jnp.concatenate([spot_ref[0]] * (WIDE // 128), 1)
            y = jnp.concatenate([spot_ref[1]] * (WIDE // 128), 1)
            turns = x * piece[0:1] + y * piece[1:2]
            turns = turns - jnp.round(turns)
            z = turns * turns
            cosine = polynomial(z, COS_TERMS)
            sine = polynomial(z, SIN_TERMS) * turns
            steering = jnp.concatenate([cosine, -sine], 0)
            s_high, s_low = halves(steering)
            weights = mm(solver_ref[local, 0], s_high) + mm(solver_ref[local, 1], s_high) + mm(solver_ref[local, 0], s_low)
            w_high, w_low = halves(weights)
            fitted = mm(turned_ref[local], w_high) + mm(turned_ref[local], w_low)
            left = steering - fitted
            power = jnp.sum(left * left, 0, keepdims=True) + ridge * jnp.sum(weights * weights, 0, keepdims=True)
            index = offset + lax.broadcasted_iota(jnp.int32, (1, WIDE), 1)
            out_ref[local : local + 1, pl.ds(offset, WIDE)] = jnp.where(index < count, LOADING * sensors / power, 0.0)
            return carry

        lax.fori_loop(0, (count + WIDE - 1) // WIDE, one_block, 0)


def exchange_kernel(devices, per_device, order_ref, snaps_ref, out_ref, send_ref, send_sem, recv_sem, own_sem):
    me = lax.axis_index("bins")
    barrier = pltpu.get_barrier_semaphore()

    def greet(step, carry):
        peer = lax.rem(me + step, devices)
        pl.semaphore_signal(barrier, inc=1, device_id={"bins": peer}, device_id_type=pl.DeviceIdType.MESH)
        return carry

    lax.fori_loop(1, devices, greet, 0)
    for owner in range(devices):
        pieces = [snaps_ref[order_ref[owner * per_device + local]].astype(F32) for local in range(per_device)]
        send_ref[owner] = jnp.concatenate(pieces, 0).astype(BF16)
    own = pltpu.make_async_copy(send_ref.at[me], out_ref.at[me], own_sem)
    own.start()
    pl.semaphore_wait(barrier, devices - 1)

    def copy(step):
        peer = lax.rem(me + step, devices)
        return pltpu.make_async_remote_copy(
            src_ref=send_ref.at[peer],
            dst_ref=out_ref.at[me],
            send_sem=send_sem.at[step],
            recv_sem=recv_sem.at[step],
            device_id={"bins": peer},
            device_id_type=pl.DeviceIdType.MESH,
        )

    def start(step, carry):
        copy(step).start()
        return carry

    def finish(step, carry):
        copy(step).wait()
        return carry

    lax.fori_loop(1, devices, start, 0)
    own.wait()
    lax.fori_loop(1, devices, finish, 0)


def few_snapshots(snapshots, directions, positions, look_counts, bin_order):
    devices = lax.axis_size("bins")
    block, total_bins, _, sensors = snapshots.shape
    per_device = total_bins // devices
    looks = directions.shape[2]
    by_bin = snapshots.reshape(block, total_bins, 2 * sensors).transpose(1, 0, 2)
    smem = pl.BlockSpec(memory_space=pltpu.SMEM)
    vmem = pl.BlockSpec(memory_space=pltpu.VMEM)
    shape = (devices, per_device * block, 2 * sensors)
    arrived = pl.pallas_call(
        functools.partial(exchange_kernel, devices, per_device),
        out_shape=jax.ShapeDtypeStruct(shape, BF16),
        in_specs=[smem, vmem],
        out_specs=vmem,
        scratch_shapes=[
            pltpu.VMEM(shape, BF16),
            pltpu.SemaphoreType.DMA((devices,)),
            pltpu.SemaphoreType.DMA((devices,)),
            pltpu.SemaphoreType.DMA,
        ],
        compiler_params=pltpu.CompilerParams(
            collective_id=0, has_side_effects=True, vmem_limit_bytes=16 * 1024 * 1024
        ),
    )(bin_order, by_bin)
    arrived = arrived.reshape(devices * per_device * block, 2 * sensors)
    snap = devices * block
    return pl.pallas_call(
        functools.partial(image_kernel, per_device, total_bins),
        out_shape=jax.ShapeDtypeStruct((per_device, looks), F32),
        in_specs=[smem, smem, vmem, vmem, vmem],
        out_specs=vmem,
        scratch_shapes=[
            pltpu.VMEM((per_device, 2, 2 * snap, 2 * sensors), BF16),
            pltpu.VMEM((per_device, 2 * sensors, 2 * snap), BF16),
            pltpu.VMEM((2, sensors, 128), F32),
        ],
        compiler_params=pltpu.CompilerParams(vmem_limit_bytes=40 * 1024 * 1024),
    )(bin_order, look_counts, arrived, directions, positions.T)


def image_bin(stacked, angles, positions, look_count, bin_id, total_bins):
    sensors = positions.shape[1]
    snap_total = stacked.shape[0]
    looks = angles.shape[1]
    products = lax.dot_general(
        stacked, stacked, (((0,), (0,)), ((), ())), preferred_element_type=jnp.float32
    )
    real_cov = (products[:sensors, :sensors] + products[sensors:, sensors:]) / snap_total
    imag_cov = (products[sensors:, :sensors] - products[:sensors, sensors:]) / snap_total
    embedded = jnp.concatenate(
        [jnp.concatenate([real_cov, -imag_cov], 1), jnp.concatenate([imag_cov, real_cov], 1)], 0
    )
    identity = jnp.eye(2 * sensors, dtype=jnp.float32)
    factor = jnp.linalg.cholesky(embedded + 0.1 * identity)
    inverse = lax.linalg.triangular_solve(factor, identity, left_side=True, lower=True)
    freq_ratio = 0.5 + (bin_id.astype(jnp.float32) + 0.5) / total_bins
    active = (look_count + LOOK_BLK - 1) // LOOK_BLK

    def one_block(block, powers):
        offset = block * LOOK_BLK
        piece = lax.dynamic_slice_in_dim(angles, offset, LOOK_BLK, 1)
        phases = (
            2.0
            * math.pi
            * freq_ratio
            * (
                positions[0][:, None] * piece[0][None, :]
                + positions[1][:, None] * piece[1][None, :]
            )
        )
        steering = jnp.concatenate([jnp.cos(phases), -jnp.sin(phases)], 0)
        whitened = jnp.dot(
            inverse, steering, precision=lax.Precision.HIGHEST, preferred_element_type=jnp.float32
        )
        quadratic = jnp.sum(whitened * whitened, 0)
        look_index = offset + jnp.arange(LOOK_BLK, dtype=jnp.int32)
        values = jnp.where(look_index < look_count, sensors / quadratic, jnp.zeros_like(quadratic))
        return lax.dynamic_update_slice_in_dim(powers, values, offset, 0)

    return lax.fori_loop(0, active, one_block, jnp.zeros((looks,), jnp.float32))


def many_snapshots(snapshots, directions, positions, look_counts, bin_order):
    devices = lax.axis_size("bins")
    device = lax.axis_index("bins")
    total_bins = snapshots.shape[1]
    per_device = total_bins // devices
    sensors = snapshots.shape[3]
    bin_ids = device * per_device + jnp.arange(per_device, dtype=jnp.int32)
    turned = lax.all_to_all(snapshots, "bins", split_axis=1, concat_axis=0, tiled=True)
    snap_total = turned.shape[0]
    rows = []
    for local in range(per_device):
        bin_id = bin_ids[local]
        stacked = turned[:, local].reshape(snap_total, 2 * sensors)
        angles = lax.dynamic_index_in_dim(directions, bin_id, 0, keepdims=False)
        look_count = lax.dynamic_index_in_dim(look_counts, bin_id, 0, keepdims=False)
        rows.append(image_bin(stacked, angles, positions, look_count, bin_id, total_bins))
    powers = jnp.stack(rows, 0)
    whole = lax.all_gather(powers, "bins", axis=0, tiled=True)
    my_rows = lax.dynamic_slice_in_dim(bin_order, device * per_device, per_device)
    powers = jnp.take(whole, my_rows, axis=0)
    return powers


def body(snapshots, directions, positions, look_counts, bin_order):
    snap_total = snapshots.shape[0] * lax.axis_size("bins")
    form = few_snapshots if snap_total < snapshots.shape[3] else many_snapshots
    return form(snapshots, directions, positions, look_counts, bin_order)


def solution(mesh):
    placed = (
        P(("groups", "bins"), None, None, None),
        P("groups", None, None),
        P(),
        P("groups"),
        P("groups"),
    )
    return jax.shard_map(
        body, mesh=mesh, in_specs=placed, out_specs=P(("groups", "bins"), None), check_vma=False
    )
```

```python
import functools
import math

import jax
import jax.numpy as jnp
from jax import lax
from jax.experimental import pallas as pl
from jax.experimental.pallas import tpu as pltpu
from jax.sharding import PartitionSpec as P

LOOK_BLK = 128
LOADING = 0.1
PIVOT = 64
WIDE = 512
COS_TERMS = (6.528658390045166, -25.967599868774414, 60.16762924194336, -85.45014190673828,
             64.93911743164062, -19.73920440673828, 1.0)
SIN_TERMS = (3.2381374835968018, -14.899847030639648, 42.02592849731445, -76.70301818847656,
             81.60513305664062, -41.34170150756836, 6.2831854820251465)
F32 = jnp.float32
BF16 = jnp.bfloat16


def mm(a, b, dims=((1,), (0,)), exact=False):
    precision = lax.Precision.HIGHEST if exact else None
    return lax.dot_general(a, b, (dims, ((), ())), precision=precision, preferred_element_type=F32)


def halves(x):
    high = x.astype(BF16)
    return high, (x - high.astype(F32)).astype(BF16)


def polynomial(z, terms):
    value = z * terms[0] + terms[1]
    for term in terms[2:]:
        value = value * z + term
    return value


def invert_small(blocks):
    n = blocks[0][0].shape[0]
    rows = lax.broadcasted_iota(jnp.int32, (n, 2 * n), 0)
    cols = lax.broadcasted_iota(jnp.int32, (n, 2 * n), 1) % n
    lane = lax.broadcasted_iota(jnp.int32, (1, 2 * n), 1)
    packed = [jnp.concatenate([re, im], 1) for re, im in blocks]
    for k in range(0, n, 2):
        pair = (cols == k) | (cols == k + 1)
        edge = pair[:1]
        for i, both in enumerate(packed):
            c0_re = jnp.broadcast_to(both[:, k : k + 1], (n, 2 * n))
            c0_im = jnp.broadcast_to(both[:, n + k : n + k + 1], (n, 2 * n))
            c1_re = jnp.broadcast_to(both[:, k + 1 : k + 2], (n, 2 * n))
            c1_im = jnp.broadcast_to(both[:, n + k + 1 : n + k + 2], (n, 2 * n))
            a, c = c0_re[k : k + 1], c1_re[k + 1 : k + 2]
            b_re, b_im = c1_re[k : k + 1], c1_im[k : k + 1]
            scale = 1.0 / (a * c - (b_re * b_re + b_im * b_im))
            a, c, b_re, b_im = a * scale, c * scale, b_re * scale, b_im * scale
            r0 = jnp.where(edge, jnp.where(lane == k, 1.0, 0.0), both[k : k + 1])
            r1 = jnp.where(edge, jnp.where(lane == k + 1, 1.0, 0.0), both[k + 1 : k + 2])
            i0 = jnp.concatenate([-r0[:, n:], r0[:, :n]], 1)
            i1 = jnp.concatenate([-r1[:, n:], r1[:, :n]], 1)
            t0 = c * r0 - (b_re * r1 + b_im * i1)
            u0 = c * i0 - (b_re * i1 - b_im * r1)
            t1 = a * r1 - (b_re * r0 - b_im * i0)
            u1 = a * i1 - (b_re * i0 + b_im * r0)
            rest = jnp.where(pair, 0.0, both) - (c0_re * t0 + c0_im * u0) - (c1_re * t1 + c1_im * u1)
            packed[i] = jnp.where(rows == k, t0, jnp.where(rows == k + 1, t1, rest))
    return [(both[:, :n], both[:, n:]) for both in packed]


def put_rows(whole, rows, start):
    stop = start + rows.shape[0]
    pieces = [rows]
    if start:
        pieces.insert(0, whole[:start])
    if stop < whole.shape[0]:
        pieces.append(whole[stop:])
    return jnp.concatenate(pieces, 0)


def invert(mats):
    n = mats[0][0].shape[0]
    mats = list(mats)
    for start in range(0, n, PIVOT):
        stop = start + PIVOT
        small = invert_small([(re[start:stop, start:stop], im[start:stop, start:stop]) for re, im in mats])
        cols = lax.broadcasted_iota(jnp.int32, (n, n), 1)
        inside = (cols >= start) & (cols < stop)
        unit = lax.broadcasted_iota(jnp.int32, (PIVOT, n), 0) + start == lax.broadcasted_iota(
            jnp.int32, (PIVOT, n), 1
        )
        band = inside[:PIVOT]
        for i, (re, im) in enumerate(mats):
            row_re = jnp.where(band, unit.astype(F32), re[start:stop])
            row_im = jnp.where(band, 0.0, im[start:stop])
            d_re, d_im = small[i]
            both = jnp.concatenate([row_re, row_im], 1)
            p = mm(d_re, both, exact=True)
            q = mm(d_im, both, exact=True)
            t_re = p[:, :n] - q[:, n:]
            t_im = p[:, n:] + q[:, :n]
            both = jnp.concatenate([t_re, t_im], 1)
            p = mm(re[:, start:stop], both, exact=True)
            q = mm(im[:, start:stop], both, exact=True)
            next_re = jnp.where(inside, 0.0, re) - p[:, :n] + q[:, n:]
            next_im = jnp.where(inside, 0.0, im) - p[:, n:] - q[:, :n]
            mats[i] = (put_rows(next_re, t_re, start), put_rows(next_im, t_im, start))
    return mats


def image_kernel(per_device, total_bins, order_ref, counts_ref, snaps_ref, directions_ref, spots_ref, out_ref,
                 solver_ref, turned_ref, spot_ref):
    first = lax.axis_index("bins") * per_device
    snap = snaps_ref.shape[0] // per_device
    sensors = spots_ref.shape[0]
    looks = out_ref.shape[1]
    ridge = LOADING * snap
    both = snaps_ref[...].astype(F32).reshape(snap // 8, per_device, 8, 2 * sensors)
    diag = lax.broadcasted_iota(jnp.int32, (snap, snap), 0) == lax.broadcasted_iota(jnp.int32, (snap, snap), 1)
    mats, fields = [], []
    for local in range(per_device):
        data = both[:, local].reshape(snap, 2 * sensors)
        turned = jnp.concatenate([-data[:, sensors:], data[:, :sensors]], 1)
        top, low = data.astype(BF16), turned.astype(BF16)
        gram_re = mm(top, top, ((1,), (1,)))
        gram_im = mm(low, top, ((1,), (1,)))
        mats.append((gram_re + jnp.where(diag, ridge, 0.0), gram_im))
        fields.append((top, low))
        turned_ref[local] = jnp.concatenate([data, turned], 0).T.astype(BF16)
    mats = invert(mats)
    for local in range(per_device):
        re, im = mats[local]
        stacked = jnp.concatenate(fields[local], 0)
        high, low = halves(jnp.concatenate([re, -im], 1))
        upper = mm(high, stacked) + mm(low, stacked)
        lower = jnp.concatenate([-upper[:, sensors:], upper[:, :sensors]], 1)
        high, low = halves(jnp.concatenate([upper, lower], 0))
        solver_ref[local, 0] = high
        solver_ref[local, 1] = low
    out_ref[...] = jnp.zeros_like(out_ref)
    for local in range(per_device):
        bin_id = order_ref[first + local]
        count = counts_ref[bin_id]
        ratio = 0.5 + (bin_id.astype(F32) + 0.5) / total_bins
        spot_ref[0] = jnp.broadcast_to(spots_ref[:, 0:1] * ratio, (sensors, 128))
        spot_ref[1] = jnp.broadcast_to(spots_ref[:, 1:2] * ratio, (sensors, 128))

        def one_block(block, carry):
            offset = pl.multiple_of(block * WIDE, WIDE)
            piece = directions_ref[bin_id, :, pl.ds(offset, WIDE)]
            x = jnp.concatenate([spot_ref[0]] * (WIDE // 128), 1)
            y = jnp.concatenate([spot_ref[1]] * (WIDE // 128), 1)
            turns = x * piece[0:1] + y * piece[1:2]
            turns = turns - jnp.round(turns)
            z = turns * turns
            cosine = polynomial(z, COS_TERMS)
            sine = polynomial(z, SIN_TERMS) * turns
            steering = jnp.concatenate([cosine, -sine], 0)
            s_high, s_low = halves(steering)
            weights = mm(solver_ref[local, 0], s_high) + mm(solver_ref[local, 1], s_high) + mm(solver_ref[local, 0], s_low)
            w_high, w_low = halves(weights)
            fitted = mm(turned_ref[local], w_high) + mm(turned_ref[local], w_low)
            left = steering - fitted
            power = jnp.sum(left * left, 0, keepdims=True) + ridge * jnp.sum(weights * weights, 0, keepdims=True)
            index = offset + lax.broadcasted_iota(jnp.int32, (1, WIDE), 1)
            out_ref[local : local + 1, pl.ds(offset, WIDE)] = jnp.where(index < count, LOADING * sensors / power, 0.0)
            return carry

        lax.fori_loop(0, (count + WIDE - 1) // WIDE, one_block, 0)


def exchange_kernel(devices, per_device, order_ref, snaps_ref, out_ref, send_ref, send_sem, recv_sem, own_sem):
    me = lax.axis_index("bins")
    barrier = pltpu.get_barrier_semaphore()

    def greet(step, carry):
        peer = lax.rem(me + step, devices)
        pl.semaphore_signal(barrier, inc=1, device_id={"bins": peer}, device_id_type=pl.DeviceIdType.MESH)
        return carry

    lax.fori_loop(1, devices, greet, 0)
    for owner in range(devices):
        pieces = [snaps_ref[order_ref[owner * per_device + local]].astype(F32) for local in range(per_device)]
        send_ref[owner] = jnp.concatenate(pieces, 0).astype(BF16)
    own = pltpu.make_async_copy(send_ref.at[me], out_ref.at[me], own_sem)
    own.start()
    pl.semaphore_wait(barrier, devices - 1)

    def copy(step):
        peer = lax.rem(me + step, devices)
        return pltpu.make_async_remote_copy(
            src_ref=send_ref.at[peer],
            dst_ref=out_ref.at[me],
            send_sem=send_sem.at[step],
            recv_sem=recv_sem.at[step],
            device_id={"bins": peer},
            device_id_type=pl.DeviceIdType.MESH,
        )

    def start(step, carry):
        copy(step).start()
        return carry

    def finish(step, carry):
        copy(step).wait()
        return carry

    lax.fori_loop(1, devices, start, 0)
    own.wait()
    lax.fori_loop(1, devices, finish, 0)


def few_snapshots(snapshots, directions, positions, look_counts, bin_order):
    devices = lax.axis_size("bins")
    block, total_bins, _, sensors = snapshots.shape
    per_device = total_bins // devices
    looks = directions.shape[2]
    by_bin = snapshots.reshape(block, total_bins, 2 * sensors).transpose(1, 0, 2)
    smem = pl.BlockSpec(memory_space=pltpu.SMEM)
    vmem = pl.BlockSpec(memory_space=pltpu.VMEM)
    shape = (devices, per_device * block, 2 * sensors)
    arrived = pl.pallas_call(
        functools.partial(exchange_kernel, devices, per_device),
        out_shape=jax.ShapeDtypeStruct(shape, BF16),
        in_specs=[smem, vmem],
        out_specs=vmem,
        scratch_shapes=[
            pltpu.VMEM(shape, BF16),
            pltpu.SemaphoreType.DMA((devices,)),
            pltpu.SemaphoreType.DMA((devices,)),
            pltpu.SemaphoreType.DMA,
        ],
        compiler_params=pltpu.CompilerParams(
            collective_id=0, has_side_effects=True, vmem_limit_bytes=16 * 1024 * 1024
        ),
    )(bin_order, by_bin)
    arrived = arrived.reshape(devices * per_device * block, 2 * sensors)
    snap = devices * block
    return pl.pallas_call(
        functools.partial(image_kernel, per_device, total_bins),
        out_shape=jax.ShapeDtypeStruct((per_device, looks), F32),
        in_specs=[smem, smem, vmem, vmem, vmem],
        out_specs=vmem,
        scratch_shapes=[
            pltpu.VMEM((per_device, 2, 2 * snap, 2 * sensors), BF16),
            pltpu.VMEM((per_device, 2 * sensors, 2 * snap), BF16),
            pltpu.VMEM((2, sensors, 128), F32),
        ],
        compiler_params=pltpu.CompilerParams(vmem_limit_bytes=40 * 1024 * 1024),
    )(bin_order, look_counts, arrived, directions, positions.T)


def image_bin(stacked, angles, positions, look_count, bin_id, total_bins):
    sensors = positions.shape[1]
    snap_total = stacked.shape[0]
    looks = angles.shape[1]
    products = lax.dot_general(
        stacked, stacked, (((0,), (0,)), ((), ())), preferred_element_type=jnp.float32
    )
    real_cov = (products[:sensors, :sensors] + products[sensors:, sensors:]) / snap_total
    imag_cov = (products[sensors:, :sensors] - products[:sensors, sensors:]) / snap_total
    embedded = jnp.concatenate(
        [jnp.concatenate([real_cov, -imag_cov], 1), jnp.concatenate([imag_cov, real_cov], 1)], 0
    )
    identity = jnp.eye(2 * sensors, dtype=jnp.float32)
    factor = jnp.linalg.cholesky(embedded + 0.1 * identity)
    inverse = lax.linalg.triangular_solve(factor, identity, left_side=True, lower=True)
    freq_ratio = 0.5 + (bin_id.astype(jnp.float32) + 0.5) / total_bins
    active = (look_count + LOOK_BLK - 1) // LOOK_BLK

    def one_block(block, powers):
        offset = block * LOOK_BLK
        piece = lax.dynamic_slice_in_dim(angles, offset, LOOK_BLK, 1)
        phases = (
            2.0
            * math.pi
            * freq_ratio
            * (
                positions[0][:, None] * piece[0][None, :]
                + positions[1][:, None] * piece[1][None, :]
            )
        )
        steering = jnp.concatenate([jnp.cos(phases), -jnp.sin(phases)], 0)
        whitened = jnp.dot(
            inverse, steering, precision=lax.Precision.HIGHEST, preferred_element_type=jnp.float32
        )
        quadratic = jnp.sum(whitened * whitened, 0)
        look_index = offset + jnp.arange(LOOK_BLK, dtype=jnp.int32)
        values = jnp.where(look_index < look_count, sensors / quadratic, jnp.zeros_like(quadratic))
        return lax.dynamic_update_slice_in_dim(powers, values, offset, 0)

    return lax.fori_loop(0, active, one_block, jnp.zeros((looks,), jnp.float32))


def many_snapshots(snapshots, directions, positions, look_counts, bin_order):
    devices = lax.axis_size("bins")
    device = lax.axis_index("bins")
    total_bins = snapshots.shape[1]
    per_device = total_bins // devices
    sensors = snapshots.shape[3]
    bin_ids = device * per_device + jnp.arange(per_device, dtype=jnp.int32)
    turned = lax.all_to_all(snapshots, "bins", split_axis=1, concat_axis=0, tiled=True)
    snap_total = turned.shape[0]
    rows = []
    for local in range(per_device):
        bin_id = bin_ids[local]
        stacked = turned[:, local].reshape(snap_total, 2 * sensors)
        angles = lax.dynamic_index_in_dim(directions, bin_id, 0, keepdims=False)
        look_count = lax.dynamic_index_in_dim(look_counts, bin_id, 0, keepdims=False)
        rows.append(image_bin(stacked, angles, positions, look_count, bin_id, total_bins))
    powers = jnp.stack(rows, 0)
    whole = lax.all_gather(powers, "bins", axis=0, tiled=True)
    my_rows = lax.dynamic_slice_in_dim(bin_order, device * per_device, per_device)
    powers = jnp.take(whole, my_rows, axis=0)
    return powers


def body(snapshots, directions, positions, look_counts, bin_order):
    snap_total = snapshots.shape[0] * lax.axis_size("bins")
    form = few_snapshots if snap_total < snapshots.shape[3] else many_snapshots
    return form(snapshots, directions, positions, look_counts, bin_order)


def solution(mesh):
    placed = (
        P(("groups", "bins"), None, None, None),
        P("groups", None, None),
        P(),
        P("groups"),
        P("groups"),
    )
    return jax.shard_map(
        body, mesh=mesh, in_specs=placed, out_specs=P(("groups", "bins"), None), check_vma=False
    )
```

```python
import functools
import math

import jax
import jax.numpy as jnp
from jax import lax
from jax.experimental import pallas as pl
from jax.experimental.pallas import tpu as pltpu
from jax.sharding import PartitionSpec as P

LOOK_BLK = 128
LOADING = 0.1
PIVOT = 64
WIDE = 512
COS_TERMS = (6.528658390045166, -25.967599868774414, 60.16762924194336, -85.45014190673828,
             64.93911743164062, -19.73920440673828, 1.0)
SIN_TERMS = (3.2381374835968018, -14.899847030639648, 42.02592849731445, -76.70301818847656,
             81.60513305664062, -41.34170150756836, 6.2831854820251465)
F32 = jnp.float32
BF16 = jnp.bfloat16


def mm(a, b, dims=((1,), (0,)), exact=False):
    precision = lax.Precision.HIGHEST if exact else None
    return lax.dot_general(a, b, (dims, ((), ())), precision=precision, preferred_element_type=F32)


def halves(x):
    high = x.astype(BF16)
    return high, (x - high.astype(F32)).astype(BF16)


def polynomial(z, terms):
    value = z * terms[0] + terms[1]
    for term in terms[2:]:
        value = value * z + term
    return value


def invert_small(blocks):
    n = blocks[0][0].shape[0]
    rows = lax.broadcasted_iota(jnp.int32, (n, n), 0)
    cols = lax.broadcasted_iota(jnp.int32, (n, n), 1)
    one_row = lax.broadcasted_iota(jnp.int32, (1, n), 1)
    blocks = list(blocks)
    for k in range(0, n, 2):
        pair = (cols == k) | (cols == k + 1)
        for i, (re, im) in enumerate(blocks):
            c0_re = jnp.broadcast_to(re[:, k : k + 1], (n, n))
            c0_im = jnp.broadcast_to(im[:, k : k + 1], (n, n))
            c1_re = jnp.broadcast_to(re[:, k + 1 : k + 2], (n, n))
            c1_im = jnp.broadcast_to(im[:, k + 1 : k + 2], (n, n))
            a, c = c0_re[k : k + 1], c1_re[k + 1 : k + 2]
            b_re, b_im = c1_re[k : k + 1], c1_im[k : k + 1]
            scale = 1.0 / (a * c - (b_re * b_re + b_im * b_im))
            a, c, b_re, b_im = a * scale, c * scale, b_re * scale, b_im * scale
            edge = (one_row == k) | (one_row == k + 1)
            r0_re = jnp.where(edge, jnp.where(one_row == k, 1.0, 0.0), re[k : k + 1])
            r1_re = jnp.where(edge, jnp.where(one_row == k, 0.0, 1.0), re[k + 1 : k + 2])
            r0_im = jnp.where(edge, 0.0, im[k : k + 1])
            r1_im = jnp.where(edge, 0.0, im[k + 1 : k + 2])
            t0_re = c * r0_re - (b_re * r1_re - b_im * r1_im)
            t0_im = c * r0_im - (b_re * r1_im + b_im * r1_re)
            t1_re = a * r1_re - (b_re * r0_re + b_im * r0_im)
            t1_im = a * r1_im - (b_re * r0_im - b_im * r0_re)
            next_re = jnp.where(pair, 0.0, re) - (c0_re * t0_re - c0_im * t0_im) - (c1_re * t1_re - c1_im * t1_im)
            next_im = jnp.where(pair, 0.0, im) - (c0_re * t0_im + c0_im * t0_re) - (c1_re * t1_im + c1_im * t1_re)
            blocks[i] = (
                jnp.where(rows == k, t0_re, jnp.where(rows == k + 1, t1_re, next_re)),
                jnp.where(rows == k, t0_im, jnp.where(rows == k + 1, t1_im, next_im)),
            )
    return blocks


def put_rows(whole, rows, start):
    stop = start + rows.shape[0]
    pieces = [rows]
    if start:
        pieces.insert(0, whole[:start])
    if stop < whole.shape[0]:
        pieces.append(whole[stop:])
    return jnp.concatenate(pieces, 0)


def invert(mats):
    n = mats[0][0].shape[0]
    mats = list(mats)
    for start in range(0, n, PIVOT):
        stop = start + PIVOT
        small = invert_small([(re[start:stop, start:stop], im[start:stop, start:stop]) for re, im in mats])
        cols = lax.broadcasted_iota(jnp.int32, (n, n), 1)
        inside = (cols >= start) & (cols < stop)
        unit = lax.broadcasted_iota(jnp.int32, (PIVOT, n), 0) + start == lax.broadcasted_iota(
            jnp.int32, (PIVOT, n), 1
        )
        band = inside[:PIVOT]
        for i, (re, im) in enumerate(mats):
            row_re = jnp.where(band, unit.astype(F32), re[start:stop])
            row_im = jnp.where(band, 0.0, im[start:stop])
            d_re, d_im = small[i]
            both = jnp.concatenate([row_re, row_im], 1)
            p = mm(d_re, both, exact=True)
            q = mm(d_im, both, exact=True)
            t_re = p[:, :n] - q[:, n:]
            t_im = p[:, n:] + q[:, :n]
            both = jnp.concatenate([t_re, t_im], 1)
            p = mm(re[:, start:stop], both, exact=True)
            q = mm(im[:, start:stop], both, exact=True)
            next_re = jnp.where(inside, 0.0, re) - p[:, :n] + q[:, n:]
            next_im = jnp.where(inside, 0.0, im) - p[:, n:] - q[:, :n]
            mats[i] = (put_rows(next_re, t_re, start), put_rows(next_im, t_im, start))
    return mats


def image_kernel(per_device, total_bins, order_ref, counts_ref, snaps_ref, directions_ref, spots_ref, out_ref,
                 solver_ref, turned_ref, spot_ref, angles_ref, angles_sem):
    first = lax.axis_index("bins") * per_device
    fetches = [
        pltpu.make_async_copy(directions_ref.at[order_ref[first + local]], angles_ref.at[local], angles_sem.at[local])
        for local in range(per_device)
    ]
    for fetch in fetches:
        fetch.start()
    snap = snaps_ref.shape[0] // per_device
    sensors = spots_ref.shape[0]
    looks = out_ref.shape[1]
    ridge = LOADING * snap
    both = snaps_ref[...].astype(F32).reshape(snap // 8, per_device, 8, 2 * sensors)
    diag = lax.broadcasted_iota(jnp.int32, (snap, snap), 0) == lax.broadcasted_iota(jnp.int32, (snap, snap), 1)
    mats, fields = [], []
    for local in range(per_device):
        data = both[:, local].reshape(snap, 2 * sensors)
        turned = jnp.concatenate([-data[:, sensors:], data[:, :sensors]], 1)
        top, low = data.astype(BF16), turned.astype(BF16)
        gram_re = mm(top, top, ((1,), (1,)))
        gram_im = mm(low, top, ((1,), (1,)))
        mats.append((gram_re + jnp.where(diag, ridge, 0.0), gram_im))
        fields.append((top, low))
        turned_ref[local] = jnp.concatenate([data, turned], 0).T.astype(BF16)
    mats = invert(mats)
    for local in range(per_device):
        re, im = mats[local]
        stacked = jnp.concatenate(fields[local], 0)
        high, low = halves(jnp.concatenate([re, -im], 1))
        upper = mm(high, stacked) + mm(low, stacked)
        lower = jnp.concatenate([-upper[:, sensors:], upper[:, :sensors]], 1)
        high, low = halves(jnp.concatenate([upper, lower], 0))
        solver_ref[local, 0] = high
        solver_ref[local, 1] = low
    out_ref[...] = jnp.zeros_like(out_ref)
    for fetch in fetches:
        fetch.wait()
    for local in range(per_device):
        bin_id = order_ref[first + local]
        count = counts_ref[bin_id]
        ratio = 0.5 + (bin_id.astype(F32) + 0.5) / total_bins
        spot_ref[0] = jnp.broadcast_to(spots_ref[:, 0:1] * ratio, (sensors, 128))
        spot_ref[1] = jnp.broadcast_to(spots_ref[:, 1:2] * ratio, (sensors, 128))

        def one_block(block, carry):
            offset = pl.multiple_of(block * WIDE, WIDE)
            piece = angles_ref[local, :, pl.ds(offset, WIDE)]
            x = jnp.concatenate([spot_ref[0]] * (WIDE // 128), 1)
            y = jnp.concatenate([spot_ref[1]] * (WIDE // 128), 1)
            turns = x * piece[0:1] + y * piece[1:2]
            turns = turns - jnp.round(turns)
            z = turns * turns
            cosine = polynomial(z, COS_TERMS)
            sine = polynomial(z, SIN_TERMS) * turns
            steering = jnp.concatenate([cosine, -sine], 0)
            s_high, s_low = halves(steering)
            weights = mm(solver_ref[local, 0], s_high) + mm(solver_ref[local, 1], s_high) + mm(solver_ref[local, 0], s_low)
            w_high, w_low = halves(weights)
            fitted = mm(turned_ref[local], w_high) + mm(turned_ref[local], w_low)
            left = steering - fitted
            power = jnp.sum(left * left, 0, keepdims=True) + ridge * jnp.sum(weights * weights, 0, keepdims=True)
            index = offset + lax.broadcasted_iota(jnp.int32, (1, WIDE), 1)
            out_ref[local : local + 1, pl.ds(offset, WIDE)] = jnp.where(index < count, LOADING * sensors / power, 0.0)
            return carry

        lax.fori_loop(0, (count + WIDE - 1) // WIDE, one_block, 0)


def exchange_kernel(devices, per_device, order_ref, snaps_ref, out_ref, send_ref, send_sem, recv_sem, own_sem):
    me = lax.axis_index("bins")
    barrier = pltpu.get_barrier_semaphore()

    def greet(step, carry):
        peer = lax.rem(me + step, devices)
        pl.semaphore_signal(barrier, inc=1, device_id={"bins": peer}, device_id_type=pl.DeviceIdType.MESH)
        return carry

    lax.fori_loop(1, devices, greet, 0)
    for owner in range(devices):
        pieces = [snaps_ref[order_ref[owner * per_device + local]].astype(F32) for local in range(per_device)]
        send_ref[owner] = jnp.concatenate(pieces, 0).astype(BF16)
    own = pltpu.make_async_copy(send_ref.at[me], out_ref.at[me], own_sem)
    own.start()
    pl.semaphore_wait(barrier, devices - 1)

    def copy(step):
        peer = lax.rem(me + step, devices)
        return pltpu.make_async_remote_copy(
            src_ref=send_ref.at[peer],
            dst_ref=out_ref.at[me],
            send_sem=send_sem.at[step],
            recv_sem=recv_sem.at[step],
            device_id={"bins": peer},
            device_id_type=pl.DeviceIdType.MESH,
        )

    def start(step, carry):
        copy(step).start()
        return carry

    def finish(step, carry):
        copy(step).wait()
        return carry

    lax.fori_loop(1, devices, start, 0)
    own.wait()
    lax.fori_loop(1, devices, finish, 0)


def few_snapshots(snapshots, directions, positions, look_counts, bin_order):
    devices = lax.axis_size("bins")
    block, total_bins, _, sensors = snapshots.shape
    per_device = total_bins // devices
    looks = directions.shape[2]
    by_bin = snapshots.reshape(block, total_bins, 2 * sensors).transpose(1, 0, 2)
    smem = pl.BlockSpec(memory_space=pltpu.SMEM)
    vmem = pl.BlockSpec(memory_space=pltpu.VMEM)
    shape = (devices, per_device * block, 2 * sensors)
    arrived = pl.pallas_call(
        functools.partial(exchange_kernel, devices, per_device),
        out_shape=jax.ShapeDtypeStruct(shape, BF16),
        in_specs=[smem, vmem],
        out_specs=vmem,
        scratch_shapes=[
            pltpu.VMEM(shape, BF16),
            pltpu.SemaphoreType.DMA((devices,)),
            pltpu.SemaphoreType.DMA((devices,)),
            pltpu.SemaphoreType.DMA,
        ],
        compiler_params=pltpu.CompilerParams(
            collective_id=0, has_side_effects=True, vmem_limit_bytes=16 * 1024 * 1024
        ),
    )(bin_order, by_bin)
    arrived = arrived.reshape(devices * per_device * block, 2 * sensors)
    snap = devices * block
    return pl.pallas_call(
        functools.partial(image_kernel, per_device, total_bins),
        out_shape=jax.ShapeDtypeStruct((per_device, looks), F32),
        in_specs=[smem, smem, vmem, pl.BlockSpec(memory_space=pl.ANY), vmem],
        out_specs=vmem,
        scratch_shapes=[
            pltpu.VMEM((per_device, 2, 2 * snap, 2 * sensors), BF16),
            pltpu.VMEM((per_device, 2 * sensors, 2 * snap), BF16),
            pltpu.VMEM((2, sensors, 128), F32),
            pltpu.VMEM((per_device, 2, looks), F32),
            pltpu.SemaphoreType.DMA((per_device,)),
        ],
        compiler_params=pltpu.CompilerParams(vmem_limit_bytes=40 * 1024 * 1024),
    )(bin_order, look_counts, arrived, directions, positions.T)


def image_bin(stacked, angles, positions, look_count, bin_id, total_bins):
    sensors = positions.shape[1]
    snap_total = stacked.shape[0]
    looks = angles.shape[1]
    products = lax.dot_general(
        stacked, stacked, (((0,), (0,)), ((), ())), preferred_element_type=jnp.float32
    )
    real_cov = (products[:sensors, :sensors] + products[sensors:, sensors:]) / snap_total
    imag_cov = (products[sensors:, :sensors] - products[:sensors, sensors:]) / snap_total
    embedded = jnp.concatenate(
        [jnp.concatenate([real_cov, -imag_cov], 1), jnp.concatenate([imag_cov, real_cov], 1)], 0
    )
    identity = jnp.eye(2 * sensors, dtype=jnp.float32)
    factor = jnp.linalg.cholesky(embedded + 0.1 * identity)
    inverse = lax.linalg.triangular_solve(factor, identity, left_side=True, lower=True)
    freq_ratio = 0.5 + (bin_id.astype(jnp.float32) + 0.5) / total_bins
    active = (look_count + LOOK_BLK - 1) // LOOK_BLK

    def one_block(block, powers):
        offset = block * LOOK_BLK
        piece = lax.dynamic_slice_in_dim(angles, offset, LOOK_BLK, 1)
        phases = (
            2.0
            * math.pi
            * freq_ratio
            * (
                positions[0][:, None] * piece[0][None, :]
                + positions[1][:, None] * piece[1][None, :]
            )
        )
        steering = jnp.concatenate([jnp.cos(phases), -jnp.sin(phases)], 0)
        whitened = jnp.dot(
            inverse, steering, precision=lax.Precision.HIGHEST, preferred_element_type=jnp.float32
        )
        quadratic = jnp.sum(whitened * whitened, 0)
        look_index = offset + jnp.arange(LOOK_BLK, dtype=jnp.int32)
        values = jnp.where(look_index < look_count, sensors / quadratic, jnp.zeros_like(quadratic))
        return lax.dynamic_update_slice_in_dim(powers, values, offset, 0)

    return lax.fori_loop(0, active, one_block, jnp.zeros((looks,), jnp.float32))


def many_snapshots(snapshots, directions, positions, look_counts, bin_order):
    devices = lax.axis_size("bins")
    device = lax.axis_index("bins")
    total_bins = snapshots.shape[1]
    per_device = total_bins // devices
    sensors = snapshots.shape[3]
    bin_ids = device * per_device + jnp.arange(per_device, dtype=jnp.int32)
    turned = lax.all_to_all(snapshots, "bins", split_axis=1, concat_axis=0, tiled=True)
    snap_total = turned.shape[0]
    rows = []
    for local in range(per_device):
        bin_id = bin_ids[local]
        stacked = turned[:, local].reshape(snap_total, 2 * sensors)
        angles = lax.dynamic_index_in_dim(directions, bin_id, 0, keepdims=False)
        look_count = lax.dynamic_index_in_dim(look_counts, bin_id, 0, keepdims=False)
        rows.append(image_bin(stacked, angles, positions, look_count, bin_id, total_bins))
    powers = jnp.stack(rows, 0)
    whole = lax.all_gather(powers, "bins", axis=0, tiled=True)
    my_rows = lax.dynamic_slice_in_dim(bin_order, device * per_device, per_device)
    powers = jnp.take(whole, my_rows, axis=0)
    return powers


def body(snapshots, directions, positions, look_counts, bin_order):
    snap_total = snapshots.shape[0] * lax.axis_size("bins")
    form = few_snapshots if snap_total < snapshots.shape[3] else many_snapshots
    return form(snapshots, directions, positions, look_counts, bin_order)


def solution(mesh):
    placed = (
        P(("groups", "bins"), None, None, None),
        P("groups", None, None),
        P(),
        P("groups"),
        P("groups"),
    )
    return jax.shard_map(
        body, mesh=mesh, in_specs=placed, out_specs=P(("groups", "bins"), None), check_vma=False
    )
```
